256 devices in a mesh: brick: 32 (over y, z), grp: 8 (over x, core).
Axes of the slice: x: 4, y: 4, z: 8, core: 2. Of those that a mesh axis runs over, the one named last changes fastest.
Arguments:
- source: float32 [4, 256, 128, 512], P(None, 'brick', 'grp'), may hold values from -35 to 80
- phase_label: int32 [256, 128, 512], P('brick', 'grp'), may hold values from 0 to 2
- interface: int32 [256, 128, 512], P('brick', 'grp'), may hold values 0 or 1
- conductivity: float32 [2, 256, 128, 512], P(None, 'brick', 'grp'), may hold values from 0.3 to 3
- admittance: float32 [2, 256, 128, 512], P(None, 'brick', 'grp'), may hold values from 0.5 to 4
- extents: int32 [32, 8], P('brick'), may hold values from 1 to 128, 512 in all within a row
- coarse_inverse: float32 [1024, 1024], P('brick'), may hold values from -1 to 4
Outputs:
- solution: float32 [4, 256, 128, 512], P(None, 'brick', 'grp')
- residual: float32 [4, 256, 128, 512], P(None, 'brick', 'grp')
The draws below stay inside these ranges and needn't reach their ends.
Inputs may be any that keep to these rules, and one draw needn't show every extreme that they name: `extents`: each brick's 8 slab lengths sum to 512; the longest is exactly 128.
All inputs are finite; a program needn't handle non-finite values. No bound on the sum of `interface` on one device may be relied on, other than what follows from the above.
Results may differ from the reference program's by a relative error of at most 0.0003.
Values sent between devices are 32-bit elements; how exact they have to be, the bound alone decides.
A program may use at most 64 MiB of HBM per device.

```python
import math
import jax
import jax.numpy as jnp
import numpy as np
from jax import lax

CX = 8
CY = 16
NZ = 512
KB = 8
ITERS = 3
MOST = 128
NX = 256
NY = 128
NC = 1024
SLAB_CELLS = 65536
N_BRICK = 32


def draw_source(key, part):
    key = jax.random.fold_in(key, 11)
    first_key = jax.random.fold_in(key, 0)
    ramp = 1.0 + 2.0 * jnp.arange(NX, dtype=jnp.float32) / max(NX - 1, 1)
    rough = jnp.clip(jax.random.normal(first_key, (4, NX, NY, NZ)), -4.0, 4.0)
    rise = 1.0 + 2.0 * jnp.arange(NY, dtype=jnp.float32) / max(NY - 1, 1)
    base = 0.5
    return ((base + rough) * rise[None, None, :, None] * ramp[None, :, None, None]).astype(jnp.float32)


def draw_coarse_inverse(key, part):
    key = jax.random.fold_in(key, 23)
    first_key, second_key = jax.random.split(key, 2)
    leading = jax.random.uniform(first_key, (NC,), minval=1.5, maxval=3.0)
    spread = jax.random.truncated_normal(second_key, -4.0, 4.0, (NC, NC)) * (0.5 / math.sqrt(NC))
    return (spread + jnp.eye(NC, dtype=jnp.float32) * leading[None, :]).astype(jnp.float32)


def touch_ends(result, stream_key, least, high):
    longest = result.shape.index(max(result.shape))
    spots = []
    for shift in (0, 1):
        where = [jax.random.randint(jax.random.fold_in(stream_key, axis), (), 0, length) for axis, length in enumerate(result.shape)]
        where[longest] = (where[longest] + shift) % result.shape[longest]
        spots.append(tuple(where))
    return result.at[spots[0]].set(least).at[spots[1]].set(high)


def steps_of(own_key, shape, cuts, low, largest):
    def one(position, shards_of):
        heights = jax.random.uniform(jax.random.fold_in(jax.random.fold_in(own_key, 6), position), (shards_of,), jnp.float32, low / len(cuts), largest / len(cuts))
        return jnp.repeat(jnp.exp(heights), shape[position] // shards_of).reshape((-1,) + (1,) * (len(shape) - position - 1))

    loudness = one(*cuts[0])
    for cut in cuts[1:]:
        loudness = loudness * one(*cut)
    return loudness


def length_profile(amount, total, reach, skew):
    weights = [(1 << 20) // math.isqrt(rank ** skew) + 1 for rank in range(2, amount + 1)]
    spare, holding = total - reach - (amount - 1), [1] * (amount - 1)
    while spare > 0:
        movable = [i for i in range(amount - 1) if holding[i] < reach]
        whole, budget = sum([weights[i] for i in movable]), spare
        for i in movable:
            more = min(reach - holding[i], max(1, budget * weights[i] // whole), spare)
            holding[i] = holding[i] + more
            spare = spare - more
    return np.array([reach] + holding)


def uneven_parts(rng, count, total, limit, lean):
    if count == 2:
        one = jax.random.randint(rng, (), max(1, total - limit), min(limit, total - 1) + 1)
        return jnp.stack([one, total - one])
    lengths = jnp.asarray(length_profile(count, total, limit, lean), jnp.int32)
    pairs = (count - 1) // 2
    source_of, receiver = lengths[1:1 + 2 * pairs:2], lengths[2:2 + 2 * pairs:2]
    room = jnp.minimum(source_of - 1, limit - receiver)
    passed = jax.random.randint(jax.random.fold_in(rng, 1), (pairs,), 0, 1 << 20) % (room + 1)
    lengths = lengths.at[1:1 + 2 * pairs:2].set(source_of - passed).at[2:2 + 2 * pairs:2].set(receiver + passed)
    return lengths[jax.random.permutation(jax.random.fold_in(rng, 2), count)]


def setup_inputs(seed: int = 0) -> dict:
    key_of = jax.random.split(jax.random.key(seed), 8)
    source = draw_source(jax.random.fold_in(key_of[7], 71), 0)
    phase_label = touch_ends(jax.random.randint(key_of[1], (NX, NY, NZ), 0, 3), jax.random.fold_in(key_of[1], 1), 0, 2).astype(jnp.int32)
    interface = touch_ends((jax.random.randint(key_of[2], (NX, NY, NZ), 0, 3) < 1).astype(jnp.int32), jax.random.fold_in(key_of[2], 1), 0, 1)
    conductivity = jnp.clip(jnp.exp(math.log(3.0) - 2.3025851 * jax.random.uniform(key_of[3], (2, NX, NY, NZ), jnp.float32) ** steps_of(key_of[3], (2, NX, NY, NZ), ((1, 32), (2, 8)), -0.2, 0.2)), 0.3, 3.0)
    admittance = jnp.clip(jnp.exp(math.log(4.0) - 2.0794415 * jax.random.uniform(key_of[4], (2, NX, NY, NZ), jnp.float32) ** steps_of(key_of[4], (2, NX, NY, NZ), ((1, 32), (2, 8)), -0.2, 0.2)), 0.5, 4.0)
    extents = jax.vmap(lambda own: uneven_parts(own, KB, NZ, MOST, 2))(jax.random.split(key_of[5], N_BRICK)).reshape((N_BRICK, KB)).astype(jnp.int32)
    coarse_inverse = draw_coarse_inverse(jax.random.fold_in(key_of[7], 71), 0)
    return {"source": source, "phase_label": phase_label, "interface": interface, "conductivity": conductivity, "admittance": admittance, "extents": extents, "coarse_inverse": coarse_inverse}


EPS_SHIFT = 0.2
LOW_COND = 0.02
PRECISE = lax.Precision.HIGHEST


def shifted(values, along, offset):
    count = values.shape[along]
    zero_shape = list(values.shape)
    zero_shape[along] = 1
    zeros = jnp.zeros(zero_shape, values.dtype)
    if offset > 0:
        return jnp.concatenate([lax.slice_in_dim(values, 1, count, axis=along), zeros], along)
    return jnp.concatenate([zeros, lax.slice_in_dim(values, 0, count - 1, axis=along)], along)


DIRECTIONS = ((1, -1), (1, 1), (2, -1), (2, 1), (3, -1), (3, 1))


def apply_operator(fields, weights, total_weight, charge_rate, storage_rate, local):
    gathered_sum = jnp.zeros_like(fields)
    xpos = jnp.arange(NX) % CX
    ypos = jnp.arange(NY) % CY
    for (along, offset), weight in zip(DIRECTIONS, weights):
        values = shifted(fields, along, offset)
        if local and along == 1:
            keep = (xpos != (CX - 1 if offset > 0 else 0)).astype(jnp.float32)
            values = values * keep[None, :, None, None]
        if local and along == 2:
            keep = (ypos != (CY - 1 if offset > 0 else 0)).astype(jnp.float32)
            values = values * keep[None, None, :, None]
        gathered_sum = gathered_sum + jnp.repeat(weight, 2, axis=0) * values
    over_real = fields[0] - fields[2]
    over_imag = fields[1] - fields[3]
    flow_real = charge_rate * over_real - storage_rate * over_imag
    flow_imag = charge_rate * over_imag + storage_rate * over_real
    coupling = jnp.stack([flow_real, flow_imag, -flow_real, -flow_imag])
    return (jnp.repeat(total_weight, 2, axis=0) + EPS_SHIFT) * fields - gathered_sum + coupling


def reference(source, phase_label, interface, conductivity, admittance, extents, coarse_inverse):
    conduct = jnp.stack([
        conductivity[0] * jnp.where(phase_label == 1, 1.0, LOW_COND),
        conductivity[1] * jnp.where(phase_label == 2, 1.0, LOW_COND)]).astype(jnp.float32)
    weights = [0.5 * (conduct + shifted(conduct, along, offset)) for along, offset in DIRECTIONS]
    total_weight = jnp.zeros_like(conduct)
    for weight in weights:
        total_weight = total_weight + weight
    mask = interface.astype(jnp.float32)
    charge_rate = admittance[0] * mask
    storage_rate = admittance[1] * mask
    diagonal = jnp.repeat(total_weight, 2, axis=0) + EPS_SHIFT + charge_rate[None]
    slab_ends = jnp.cumsum(extents, axis=1).astype(jnp.int32)
    starts = slab_ends - extents
    depth = jnp.arange(NZ).astype(jnp.int32)
    onehot = ((depth[None, :, None] >= starts[:, None, :]) & (depth[None, :, None] < slab_ends[:, None, :])).astype(jnp.float32)

    def restrict(values):
        plane = values.reshape(4, N_BRICK, CX * NY, NZ).sum(axis=2)
        coarse = jnp.einsum('fbz,bzk->bfk', plane, onehot, precision=PRECISE) / SLAB_CELLS
        return coarse.reshape(NC)

    def prolong(coarse):
        correction = jnp.dot(coarse_inverse, coarse, precision=PRECISE).reshape(N_BRICK, 4, KB)
        profile = jnp.einsum('bfk,bzk->fbz', correction, onehot, precision=PRECISE)
        return jnp.broadcast_to(profile[:, :, None, None, :], (4, N_BRICK, CX, NY, NZ)).reshape(4, NX, NY, NZ)

    solution = jnp.zeros_like(source)
    residual = source.astype(jnp.float32)
    for iteration in range(ITERS):
        coarse = restrict(residual)
        first = residual / diagonal
        second = first + (residual - apply_operator(first, weights, total_weight, charge_rate, storage_rate, True)) / diagonal
        search = second + prolong(coarse)
        image = apply_operator(search, weights, total_weight, charge_rate, storage_rate, False)
        alpha = jnp.sum(residual * image) / (jnp.sum(image * image) + 1e-6)
        solution = solution + alpha * search
        residual = residual - alpha * image
    return solution, residual
```

```python
import jax
import jax.numpy as jnp
from jax import lax
from jax.experimental import pallas as pl
from jax.experimental.pallas import tpu as pltpu
from jax.sharding import PartitionSpec as P

CX, CY, NZ, KB = 8, 16, 512, 8
ITERS = 3
SLAB_CELLS = 65536.0
EPS_SHIFT = 0.2
LOW_COND = 0.02
LANES = 128
TILES = NZ // LANES
MESH = pl.DeviceIdType.MESH
F32 = jnp.float32


def roll(v, shift, axis):
    return pltpu.roll(v, shift % v.shape[axis], axis)


def kernel(
    ext, src_h, phase_h, inter_h, cond_h, adm_h, cinv_h, sol_h, res_h,
    r, q, u, z, sol, first, second, cond, phase, inter, adm, cd, cr, sr,
    wx, wym, wyp, wzm, wzp, tw, ee, dinv, wyb, cinv, onehot, table,
    hxc, hyc, syc, hx, hy, sy, row_g, slots_g, slots_y, slots_z, row_c, slots_c, row_all, slots_all, sizes,
    load_sem, out_sem, near_send, near_recv, c_sem, halo_sem, p0_send, p0_recv, core_sem, all_send, all_recv,
):
    brick, grp = lax.axis_index("brick"), lax.axis_index("grp")
    cy, cz, cx, core = brick // 8, brick % 8, grp // 2, grp % 2
    up = {"brick": (brick + 1) % 32, "grp": grp}
    down = {"brick": (brick + 31) % 32, "grp": grp}
    right = {"brick": brick, "grp": (grp + 1) % 8}
    left = {"brick": brick, "grp": (grp + 7) % 8}
    group = [{"brick": brick, "grp": (grp + j) % 8} for j in (4, 5, 3, 2, 6, 1, 7)]
    along_y = [{"brick": ((cy + j) % 4) * 8 + cz, "grp": grp} for j in (2, 1, 3)]
    along_z = [{"brick": cy * 8 + (cz + j) % 8, "grp": grp} for j in (4, 3, 5, 2, 6, 1, 7)]

    def load(n, a, b):
        return pltpu.make_async_copy(a, b, load_sem.at[n])

    loads = [
        load(0, cond_h, cond), load(1, phase_h, phase), load(2, src_h, r),
        load(3, cinv_h, cinv.at[1]), load(4, inter_h, inter), load(5, adm_h, adm),
    ]
    for copy in loads:
        copy.start()
    barrier = pltpu.get_barrier_semaphore()
    greeted = along_z + group + along_y + [up, down]
    for dev in greeted:
        pl.semaphore_signal(barrier, inc=1, device_id=dev, device_id_type=MESH)

    lane = lax.broadcasted_iota(jnp.int32, (8, LANES), 1)
    sub = lax.broadcasted_iota(jnp.int32, (8, LANES), 0)
    slab_row = lax.broadcasted_iota(jnp.int32, (CY, NZ), 0)
    slab_col = lax.broadcasted_iota(jnp.int32, (CY, NZ), 1)
    base = (brick % 4) * 32

    def remote(a, b, send, recv, dev):
        return pltpu.make_async_remote_copy(
            src_ref=a, dst_ref=b, send_sem=send, recv_sem=recv, device_id=dev, device_id_type=MESH
        )

    def await_bytes(ref, sem):
        pltpu.make_async_copy(ref, ref, sem).wait()

    depth = lax.broadcasted_iota(jnp.int32, (KB, NZ), 1)
    slab = lax.broadcasted_iota(jnp.int32, (KB, NZ), 0)
    start = jnp.int32(0)
    begins = jnp.zeros((KB, NZ), jnp.int32)
    ends = jnp.zeros((KB, NZ), jnp.int32)
    for k in range(KB):
        stop = start + ext[0, k]
        begins = jnp.where(slab == k, start, begins)
        ends = jnp.where(slab == k, stop, ends)
        start = stop
    own_onehot = jnp.where((depth >= begins) & (depth < ends), 1.0, 0.0).astype(F32)
    onehot[1] = own_onehot

    def restrict_row(planes):
        spread = jnp.zeros((8, LANES), F32)
        for f in range(4):
            total = jnp.sum(planes[f], axis=0, keepdims=True)
            value = jnp.sum(total * onehot[1], axis=1, keepdims=True)
            spread = spread + jnp.where(lane == base + 8 * f + sub, value, 0.0)
        return jnp.sum(spread, axis=0, keepdims=True) * (1.0 / SLAB_CELLS)

    loads[0].wait()
    loads[1].wait()

    def masked(x, carry):
        for i in range(2):
            value = cond[i, x] * jnp.where(phase[x] == i + 1, 1.0, LOW_COND)
            cd[i, x + 1] = value
            syc[0, i, pl.ds(x, 1), :] = value[0:1]
            syc[1, i, pl.ds(x, 1), :] = value[CY - 1 : CY]
        return carry

    lax.fori_loop(0, CX, masked, 0)

    loads[2].wait()

    def plane_of(x, carry):
        return tuple(carry[f] + r[f, x, 0:8] + r[f, x, 8:16] for f in range(4))

    planes = lax.fori_loop(0, CX, plane_of, tuple(jnp.zeros((8, NZ), F32) for _ in range(4)))
    row_g[0:1] = restrict_row(planes)
    loads[3].wait()

    pl.semaphore_wait(barrier, len(greeted))

    started = []

    def go(copy):
        copy.start()
        started.append(copy)
        return copy

    for dev in group:
        remote(row_g.at[pl.ds(0, 1)], slots_g.at[pl.ds(grp, 1)], p0_send.at[0], p0_recv.at[0], dev).start()
    pltpu.make_async_copy(row_g.at[pl.ds(0, 1)], slots_g.at[pl.ds(grp, 1)], p0_recv.at[0]).start()
    cond_up = go(remote(cd.at[:, CX], hxc.at[0], near_send.at[0], near_recv.at[0], up))
    cond_down = go(remote(cd.at[:, 1], hxc.at[1], near_send.at[1], near_recv.at[1], down))
    cond_right = go(remote(syc.at[1], hyc.at[0], near_send.at[2], near_recv.at[2], right))
    cond_left = go(remote(syc.at[0], hyc.at[1], near_send.at[3], near_recv.at[3], left))
    hot_up = go(remote(onehot.at[1], onehot.at[0], near_send.at[4], near_recv.at[4], up))
    hot_down = go(remote(onehot.at[1], onehot.at[2], near_send.at[5], near_recv.at[5], down))
    cinv_up = go(remote(cinv.at[1], cinv.at[0], near_send.at[6], near_recv.at[6], up))
    cinv_down = go(remote(cinv.at[1], cinv.at[2], near_send.at[7], near_recv.at[7], down))

    loads[4].wait()
    loads[5].wait()

    def rates(x, carry):
        mask = inter[x].astype(F32)
        cr[x] = adm[0, x] * mask
        sr[x] = adm[1, x] * mask
        return carry

    lax.fori_loop(0, CX, rates, 0)
    for f in range(4):
        for edge in (0, CX + 1):
            first[f, edge] = jnp.zeros((CY, NZ), F32)
            second[0, f, edge] = jnp.zeros((CY, NZ), F32)
            second[1, f, edge] = jnp.zeros((CY, NZ), F32)

    await_bytes(slots_g, p0_recv.at[0])
    row_g[8:9] = jnp.sum(slots_g[...], axis=0, keepdims=True)
    for dev in along_y:
        remote(row_g.at[pl.ds(8, 1)], slots_y.at[pl.ds(cy, 1)], p0_send.at[1], p0_recv.at[1], dev).start()
    pltpu.make_async_copy(row_g.at[pl.ds(8, 1)], slots_y.at[pl.ds(cy, 1)], p0_recv.at[1]).start()

    inside = [
        jnp.where(brick > 0, 1.0, 0.0).astype(F32), jnp.where(brick < 31, 1.0, 0.0).astype(F32),
        jnp.where(grp > 0, 1.0, 0.0).astype(F32), jnp.where(grp < 7, 1.0, 0.0).astype(F32),
    ]
    for copy in (cond_up, cond_down, cond_right, cond_left):
        copy.wait_recv()
    for i in range(2):
        cd[i, 0] = hxc[0, i] * inside[0]
        cd[i, CX + 1] = hxc[1, i] * inside[1]

    def weigh(x, carry):
        out_low = jnp.where((x == 0) & (brick == 0), 1.0, 0.0).astype(F32)
        out_high = jnp.where((x == CX - 1) & (brick == 31), 1.0, 0.0).astype(F32)
        charge = cr[x]
        for i in range(2):
            here = cd[i, x + 1]
            low = 0.5 * (here + cd[i, x])
            high = 0.5 * (here + cd[i, x + 2])
            before = hyc[0, i, pl.ds(x, 1), :] * inside[2]
            after = hyc[1, i, pl.ds(x, 1), :] * inside[3]
            ym = 0.5 * (here + jnp.where(slab_row == 0, before, roll(here, 1, 0)))
            yp = 0.5 * (here + jnp.where(slab_row == CY - 1, after, roll(here, -1, 0)))
            zm = 0.5 * (here + jnp.where(slab_col == 0, 0.0, roll(here, 1, 1)))
            zp = 0.5 * (here + jnp.where(slab_col == NZ - 1, 0.0, roll(here, -1, 1)))
            total = low + high + ym + yp + zm + zp + EPS_SHIFT
            tw[i, x] = total
            dinv[i, x] = 1.0 / (total + charge)
            ee[i, x] = (
                EPS_SHIFT + zm + zp + out_low * low + out_high * high
                + jnp.where(slab_row == 0, ym, 0.0) * (1.0 - inside[2])
                + jnp.where(slab_row == CY - 1, yp, 0.0) * (1.0 - inside[3])
            )
            wx[i, x] = low * (1.0 - out_low)
            wx[i, x + 1] = high * (1.0 - out_high)
            wyb[0, i, pl.ds(x, 1), :] = ym[0:1] * inside[2]
            wyb[1, i, pl.ds(x, 1), :] = yp[CY - 1 : CY] * inside[3]
            wym[i, x] = jnp.where(slab_row == 0, 0.0, ym)
            wyp[i, x] = jnp.where(slab_row == CY - 1, 0.0, yp)
            wzm[i, x] = jnp.where(slab_col == 0, 0.0, zm)
            wzp[i, x] = jnp.where(slab_col == NZ - 1, 0.0, zp)
        return carry

    lax.fori_loop(0, CX, weigh, 0)

    def around(v, f, x, center):
        i = f // 2
        return (
            wx[i, x] * v[f, x] + wx[i, x + 1] * v[f, x + 2]
            + wym[i, x] * roll(center, 1, 0) + wyp[i, x] * roll(center, -1, 0)
            + wzm[i, x] * roll(center, 1, 1) + wzp[i, x] * roll(center, -1, 1)
        )

    def smooth(given, k):
        out = second.at[k % 2]

        def scaled(x, carry):
            for f in range(4):
                first[f, x + 1] = given[f, x] * dinv[f // 2, x]
            return carry

        lax.fori_loop(0, CX, scaled, 0)

        def stencil(x, carry):
            v = [first[f, x + 1] for f in range(4)]
            real, imag = sr[x] * (v[0] - v[2]), sr[x] * (v[1] - v[3])
            swirl = (imag, -real, -imag, real)
            for f in range(4):
                value = v[f] + dinv[f // 2, x] * (around(first, f, x, v[f]) + cr[x] * v[f ^ 2] + swirl[f])
                out[f, x + 1] = value
                sy[k, 0, f, pl.ds(x, 1), :] = value[0:1]
                sy[k, 1, f, pl.ds(x, 1), :] = value[CY - 1 : CY]
            return carry

        lax.fori_loop(0, 2, lambda n, c: stencil(n * (CX - 1), c), 0)
        halos = [
            remote(out.at[:, CX], hx.at[k, 0], halo_sem.at[k, 0, 0], halo_sem.at[k, 1, 0], up),
            remote(out.at[:, 1], hx.at[k, 1], halo_sem.at[k, 0, 1], halo_sem.at[k, 1, 1], down),
        ]
        for copy in halos:
            copy.start()
        lax.fori_loop(1, CX - 1, stencil, 0)
        sides = [
            remote(sy.at[k, 1], hy.at[k, 0], halo_sem.at[k, 0, 2], halo_sem.at[k, 1, 2], right),
            remote(sy.at[k, 0], hy.at[k, 1], halo_sem.at[k, 0, 3], halo_sem.at[k, 1, 3], left),
        ]
        for copy in sides:
            copy.start()
        return halos + sides

    def operate(k):
        v = second.at[k % 2]

        def stencil(x, carry):
            c = [v[f, x + 1] for f in range(4)]
            over_real, over_imag = c[0] - c[2], c[1] - c[3]
            real = cr[x] * over_real - sr[x] * over_imag
            imag = cr[x] * over_imag + sr[x] * over_real
            flow = (real, imag, -real, -imag)
            for f in range(4):
                u[f, x] = tw[f // 2, x] * c[f] - around(v, f, x, c[f]) + flow[f]
            return carry

        lax.fori_loop(0, CX, stencil, 0)

    def receive_halos(k, copies):
        for copy in copies:
            copy.wait_recv()
        for f in range(4):
            u[f, 0] = u[f, 0] - wx[f // 2, 0] * hx[k, 0, f]
            u[f, CX - 1] = u[f, CX - 1] - wx[f // 2, CX] * hx[k, 1, f]

        def rows(x, carry):
            for f in range(4):
                for side, y in ((0, 0), (1, CY - 1)):
                    u[f, x, y : y + 1, :] = u[f, x, y : y + 1, :] - (
                        wyb[side, f // 2, pl.ds(x, 1), :] * hy[k, side, f, pl.ds(x, 1), :]
                    )
            return carry

        lax.fori_loop(0, CX, rows, 0)
        for copy in copies:
            copy.wait_send()

    def correct(coarse):
        profile = []
        for j in range(3):
            per_field = []
            for f in range(4):
                product = jnp.zeros((8, LANES), F32)
                for s in range(8):
                    product = product + cinv[j, 8 * f : 8 * f + 8, LANES * s : LANES * s + LANES] * coarse[s]
                value = jnp.sum(product, axis=1, keepdims=True)
                per_field.append(jnp.sum(value * onehot[j], axis=0, keepdims=True))
            profile.append(per_field)
        own = profile[1]
        rows = own + [roll(own[f], 1, 1) for f in range(4)] + [roll(own[f], -1, 1) for f in range(4)]
        rows = rows + [own[0] - own[2], own[1] - own[3]]
        for n, value in enumerate(rows):
            table[n] = jnp.broadcast_to(value, (8, NZ))
        for f in range(4):
            u[f, 0] = u[f, 0] - wx[f // 2, 0] * (profile[0][f] - own[f])
            u[f, CX - 1] = u[f, CX - 1] - wx[f // 2, CX] * (profile[2][f] - own[f])

    def advance(k, alpha):
        zero = jnp.zeros((8, LANES), F32)
        ri, ii = zero, zero
        planes = [[] for _ in range(4)]
        for t in range(TILES):
            lanes = slice(LANES * t, LANES * (t + 1))
            p = [table[n, :, lanes] for n in range(14)]

            def step(x, carry):
                ri, ii, *sums = carry
                for half in range(2):
                    at = (x, slice(8 * half, 8 * half + 8), lanes)
                    charge, storage = cr[at], sr[at]
                    real = charge * p[12] - storage * p[13]
                    imag = charge * p[13] + storage * p[12]
                    flow = (real, imag, -real, -imag)
                    for f in range(4):
                        i = f // 2
                        raised = u[(f,) + at] + (
                            ee[(i,) + at] * p[f] - wzm[(i,) + at] * p[4 + f] - wzp[(i,) + at] * p[8 + f] + flow[f]
                        )
                        left_over = r[(f,) + at]
                        if k > 0:
                            old = q[(f,) + at]
                            left_over = left_over - alpha * old
                            r[(f,) + at] = left_over
                            raised = old - alpha * raised
                        q[(f,) + at] = raised
                        ri = ri + left_over * raised
                        ii = ii + raised * raised
                        sums[f] = sums[f] + raised
                return (ri, ii, *sums)

            ri, ii, *sums = lax.fori_loop(0, CX, step, (ri, ii, zero, zero, zero, zero))
            for f in range(4):
                planes[f].append(sums[f])
        return ri, ii, [jnp.concatenate(parts, axis=1) for parts in planes]

    def update_search(k, alpha):
        smoothed = second.at[k % 2]

        def step(x, carry):
            for f in range(4):
                put = smoothed[f, x + 1] + jnp.concatenate([table[f], table[f]], axis=0)
                if k == 0:
                    z[f, x] = put
                else:
                    old = z[f, x]
                    sol[f, x] = alpha * old if k == 1 else sol[f, x] + alpha * old
                    z[f, x] = old - alpha * put
            return carry

        lax.fori_loop(0, CX, step, 0)

    slot = cx * 32 + (cz % 4) * 8 + (cz // 4) * 4 + cy
    ys = [((cy + j) % 4) * 8 for j in range(4)]
    xs = [((cx + j) % 4) * 2 + core for j in range(4)]
    far_first = [2, 1, 3, 0]
    plane_order = [(dy, dx) for dy in far_first for dx in far_first]
    plane_order.sort(key=lambda p: -min(p[0], 4 - p[0]) - min(p[1], 4 - p[1]))
    sibling = {"brick": brick, "grp": cx * 2 + 1 - core}

    def share(k, ri, ii, planes):
        coarse = restrict_row(planes)
        ri = jnp.sum(jnp.sum(ri, axis=0, keepdims=True), axis=1, keepdims=True)
        ii = jnp.sum(jnp.sum(ii, axis=0, keepdims=True), axis=1, keepdims=True)
        row_c[k, 0:1, 0:LANES] = coarse
        row_c[k, 0:1, LANES : 2 * LANES] = jnp.where(lane[0:1] < 64, ri, ii)
        copy = remote(row_c.at[k], slots_c.at[k], core_sem.at[k, 0], core_sem.at[k, 1], sibling)
        copy.start()
        copy.wait_recv()
        both = row_c[k, 0:1] + slots_c[k, 0:1]
        row_all[k, 0:1] = both

        def send(by, bx):
            remote(
                row_all.at[k, pl.ds(0, 1)], slots_all.at[k, pl.ds(slot, 1)], all_send.at[k], all_recv.at[k],
                {"brick": by, "grp": bx},
            ).start()

        def far(n, carry):
            half = (n + 1) // 2
            dz = 4 + half * (1 - 2 * (n % 2))
            bz = (cz + dz) % 8
            for dy, dx in plane_order:
                send(ys[dy] + bz, xs[dx])
            return carry

        lax.fori_loop(0, 7, far, 0)
        for dy, dx in plane_order[:-1]:
            send(ys[dy] + cz, xs[dx])
        pltpu.make_async_copy(
            row_all.at[k, pl.ds(0, 1)], slots_all.at[k, pl.ds(slot, 1)], all_recv.at[k]
        ).start()
        return copy

    def gather(k):
        await_bytes(slots_all.at[k], all_recv.at[k])
        rows = slots_all[k, 0:8]
        for n in range(1, 16):
            rows = rows + slots_all[k, 8 * n : 8 * n + 8]
        dots = jnp.sum(rows[:, LANES:], axis=0, keepdims=True)
        other = roll(dots, 64, 1)
        ri = jnp.where(lane[0:1] < 64, dots, other)
        ii = jnp.where(lane[0:1] < 64, other, dots)
        return rows[:, :LANES], ri / (ii + 1e-6)

    def coarse_rows(rows):
        return [rows[4 * (s % 2) + s // 2 : 4 * (s % 2) + s // 2 + 1] for s in range(8)]

    halos = smooth(r, 0)

    await_bytes(slots_y, p0_recv.at[1])
    slots_z[pl.ds(cz, 1)] = slots_y[...][None]
    for dev in along_z:
        remote(slots_y, slots_z.at[cz], p0_send.at[2], p0_recv.at[2], dev).start()

    operate(0)
    receive_halos(0, halos)
    for copy in (hot_up, hot_down, cinv_up, cinv_down):
        copy.wait_recv()
    await_bytes(slots_z.at[pl.ds(0, 7)], p0_recv.at[2])
    low = slots_z[0] + slots_z[1] + slots_z[2] + slots_z[3]
    high = slots_z[4] + slots_z[5] + slots_z[6] + slots_z[7]
    rows = jnp.concatenate([low, high], axis=0)
    alpha = None
    cores = []
    for k in range(ITERS):
        correct(coarse_rows(rows))
        ri, ii, planes = advance(k, None if k == 0 else jnp.broadcast_to(alpha, (8, LANES)))
        cores.append(share(k, ri, ii, planes))
        wide = None if k == 0 else jnp.broadcast_to(jnp.concatenate([alpha] * TILES, axis=1), (CY, NZ))
        if k < ITERS - 1:
            halos = smooth(q, k + 1)
        update_search(k, wide)
        if k < ITERS - 1:
            operate(k + 1)
            receive_halos(k + 1, halos)
        rows, alpha = gather(k)

    wide = jnp.broadcast_to(jnp.concatenate([alpha] * TILES, axis=1), (CY, NZ))

    def finish(x, carry):
        for f in range(4):
            sol[f, x] = sol[f, x] + wide * z[f, x]
            r[f, x] = r[f, x] - wide * q[f, x]
        return carry

    lax.fori_loop(0, CX, finish, 0)
    outs = [pltpu.make_async_copy(sol, sol_h, out_sem.at[0]), pltpu.make_async_copy(r, res_h, out_sem.at[1])]
    for copy in outs:
        copy.start()
    for copy in started + cores:
        copy.wait_send()
    await_bytes(sizes.at[pl.ds(0, 7), :, pl.ds(0, LANES)], p0_send.at[0])
    await_bytes(sizes.at[pl.ds(0, 3), :, pl.ds(0, LANES)], p0_send.at[1])
    await_bytes(slots_z.at[pl.ds(0, 7)], p0_send.at[2])
    for k in range(ITERS):
        await_bytes(sizes, all_send.at[k])
    for copy in outs:
        copy.wait()


def local(source, phase_label, interface, conductivity, admittance, extents, coarse_inverse):
    block = (CX, CY, NZ)
    padded = (CX + 2, CY, NZ)
    vmem = lambda *shape: pltpu.VMEM(shape, F32)
    ints = pltpu.VMEM(block, jnp.int32)
    dma = lambda *shape: pltpu.SemaphoreType.DMA(shape)
    scratch = [
        vmem(4, *block), vmem(4, *block), vmem(4, *block), vmem(4, *block), vmem(4, *block),
        vmem(4, *padded), vmem(2, 4, *padded), vmem(2, *block), ints, ints, vmem(2, *block),
        vmem(2, *padded), vmem(*block), vmem(*block),
        vmem(2, CX + 1, CY, NZ), vmem(2, *block), vmem(2, *block), vmem(2, *block), vmem(2, *block),
        vmem(2, *block), vmem(2, *block), vmem(2, *block), vmem(2, 2, CX, NZ),
        vmem(3, 4 * KB, 1024), vmem(3, KB, NZ), vmem(14, 8, NZ),
        vmem(2, 2, CY, NZ), vmem(2, 2, CX, NZ), vmem(2, 2, CX, NZ),
        vmem(3, 2, 4, CY, NZ), vmem(3, 2, 4, CX, NZ), vmem(3, 2, 4, CX, NZ),
        vmem(16, LANES), vmem(8, LANES), vmem(4, LANES), vmem(8, 4, LANES),
        vmem(3, 1, 2 * LANES), vmem(3, 1, 2 * LANES), vmem(3, 1, 2 * LANES), vmem(3, 128, 2 * LANES),
        vmem(127, 1, 2 * LANES),
        dma(6), dma(2), dma(8), dma(8), dma(1), dma(3, 2, 4), dma(3), dma(3), dma(3, 2), dma(3), dma(3),
    ]
    hbm = pl.BlockSpec(memory_space=pl.ANY)
    out = jax.ShapeDtypeStruct((4, *block), F32)
    return pl.pallas_call(
        kernel,
        out_shape=(out, out),
        in_specs=[pl.BlockSpec(memory_space=pltpu.SMEM)] + [hbm] * 6,
        out_specs=(hbm, hbm),
        scratch_shapes=scratch,
        compiler_params=pltpu.CompilerParams(
            collective_id=0, has_side_effects=True, vmem_limit_bytes=48 * 1024 * 1024
        ),
    )(extents, source, phase_label, interface, conductivity, admittance, coarse_inverse)


def solution(mesh):
    placed = (
        P(None, "brick", "grp", None),
        P("brick", "grp", None),
        P("brick", "grp", None),
        P(None, "brick", "grp", None),
        P(None, "brick", "grp", None),
        P("brick", None),
        P("brick", None),
    )
    return jax.shard_map(
        local,
        mesh=mesh,
        in_specs=placed,
        out_specs=(P(None, "brick", "grp", None), P(None, "brick", "grp", None)),
        check_vma=False,
    )
```

```python
import jax
import jax.numpy as jnp
from jax import lax
from jax.experimental import pallas as pl
from jax.experimental.pallas import tpu as pltpu
from jax.sharding import PartitionSpec as P

CX, CY, NZ, KB = 8, 16, 512, 8
ITERS = 3
SLAB_CELLS = 65536.0
EPS_SHIFT = 0.2
LOW_COND = 0.02
LANES = 128
TILES = NZ // LANES
MESH = pl.DeviceIdType.MESH
F32 = jnp.float32


def roll(v, shift, axis):
    return pltpu.roll(v, shift % v.shape[axis], axis)


def kernel(
    ext, src_h, phase_h, inter_h, cond_h, adm_h, cinv_h, sol_h, res_h,
    r, q, u, z, sol, first, second, cond, phase, inter, adm, cd, cr, sr,
    wx, wym, wyp, wzm, wzp, tw, ee, dinv, wyb, cinv, onehot, table,
    hxc, hyc, syc, hx, hy, sy, row_z, slots_z, row_p, slots_p, row_c, slots_c, row_all, slots_all, sizes,
    load_sem, out_sem, near_send, near_recv, c_sem, halo_sem, p0_send, p0_recv, core_sem, all_send, all_recv,
):
    brick, grp = lax.axis_index("brick"), lax.axis_index("grp")
    cy, cz, cx, core = brick // 8, brick % 8, grp // 2, grp % 2
    up = {"brick": (brick + 1) % 32, "grp": grp}
    down = {"brick": (brick + 31) % 32, "grp": grp}
    right = {"brick": brick, "grp": (grp + 1) % 8}
    left = {"brick": brick, "grp": (grp + 7) % 8}
    ys = [((cy + j) % 4) * 8 for j in range(4)]
    xs = [((cx + j) % 4) * 2 for j in range(4)]
    far_first = [(dy, dx) for dy in (2, 1, 3, 0) for dx in (2, 1, 3, 0)]
    far_first.sort(key=lambda p: -min(p[0], 4 - p[0]) - min(p[1], 4 - p[1]))
    plane = [
        {"brick": ys[dy] + cz, "grp": xs[dx] + (core if same else 1 - core)}
        for dy, dx in far_first for same in (0, 1) if (dy, dx, same) != (0, 0, 1)
    ]
    along_z = [{"brick": cy * 8 + (cz + j) % 8, "grp": grp} for j in (4, 3, 5, 2, 6, 1, 7)]

    def load(n, a, b):
        return pltpu.make_async_copy(a, b, load_sem.at[n])

    loads = [
        load(0, cond_h, cond), load(1, phase_h, phase), load(2, src_h, r),
        load(3, cinv_h, cinv.at[1]), load(4, inter_h, inter), load(5, adm_h, adm),
    ]
    for copy in loads:
        copy.start()
    barrier = pltpu.get_barrier_semaphore()
    greeted = along_z + plane + [up, down]
    for dev in greeted:
        pl.semaphore_signal(barrier, inc=1, device_id=dev, device_id_type=MESH)

    lane = lax.broadcasted_iota(jnp.int32, (8, LANES), 1)
    sub = lax.broadcasted_iota(jnp.int32, (8, LANES), 0)
    slab_row = lax.broadcasted_iota(jnp.int32, (CY, NZ), 0)
    slab_col = lax.broadcasted_iota(jnp.int32, (CY, NZ), 1)
    base = (cz % 4) * 32

    def remote(a, b, send, recv, dev):
        return pltpu.make_async_remote_copy(
            src_ref=a, dst_ref=b, send_sem=send, recv_sem=recv, device_id=dev, device_id_type=MESH
        )

    def await_bytes(ref, sem):
        pltpu.make_async_copy(ref, ref, sem).wait()

    depth = lax.broadcasted_iota(jnp.int32, (KB, NZ), 1)
    slab = lax.broadcasted_iota(jnp.int32, (KB, NZ), 0)
    start = jnp.int32(0)
    begins = jnp.zeros((KB, NZ), jnp.int32)
    ends = jnp.zeros((KB, NZ), jnp.int32)
    for k in range(KB):
        stop = start + ext[0, k]
        begins = jnp.where(slab == k, start, begins)
        ends = jnp.where(slab == k, stop, ends)
        start = stop
    own_onehot = jnp.where((depth >= begins) & (depth < ends), 1.0, 0.0).astype(F32)
    onehot[1] = own_onehot

    def restrict_row(planes, base):
        spread = jnp.zeros((8, LANES), F32)
        for f in range(4):
            total = jnp.sum(planes[f], axis=0, keepdims=True)
            value = jnp.sum(total * onehot[1], axis=1, keepdims=True)
            spread = spread + jnp.where(lane == base + 8 * f + sub, value, 0.0)
        return jnp.sum(spread, axis=0, keepdims=True) * (1.0 / SLAB_CELLS)

    loads[0].wait()
    loads[1].wait()

    def masked(x, carry):
        for i in range(2):
            value = cond[i, x] * jnp.where(phase[x] == i + 1, 1.0, LOW_COND)
            cd[i, x + 1] = value
            syc[0, i, pl.ds(x, 1), :] = value[0:1]
            syc[1, i, pl.ds(x, 1), :] = value[CY - 1 : CY]
        return carry

    lax.fori_loop(0, CX, masked, 0)

    loads[2].wait()

    def plane_of(x, carry):
        return tuple(carry[f] + r[f, x, 0:8] + r[f, x, 8:16] for f in range(4))

    planes = lax.fori_loop(0, CX, plane_of, tuple(jnp.zeros((8, NZ), F32) for _ in range(4)))
    row_z[...] = restrict_row(planes, base)
    loads[3].wait()

    pl.semaphore_wait(barrier, len(greeted))

    started = []

    def go(copy):
        copy.start()
        started.append(copy)
        return copy

    for dev in along_z:
        remote(row_z, slots_z.at[pl.ds(cz, 1)], p0_send.at[0], p0_recv.at[0], dev).start()
    pltpu.make_async_copy(row_z, slots_z.at[pl.ds(cz, 1)], p0_recv.at[0]).start()
    cond_up = go(remote(cd.at[:, CX], hxc.at[0], near_send.at[0], near_recv.at[0], up))
    cond_down = go(remote(cd.at[:, 1], hxc.at[1], near_send.at[1], near_recv.at[1], down))
    cond_right = go(remote(syc.at[1], hyc.at[0], near_send.at[2], near_recv.at[2], right))
    cond_left = go(remote(syc.at[0], hyc.at[1], near_send.at[3], near_recv.at[3], left))
    hot_up = go(remote(onehot.at[1], onehot.at[0], near_send.at[4], near_recv.at[4], up))
    hot_down = go(remote(onehot.at[1], onehot.at[2], near_send.at[5], near_recv.at[5], down))
    cinv_up = go(remote(cinv.at[1], cinv.at[0], near_send.at[6], near_recv.at[6], up))
    cinv_down = go(remote(cinv.at[1], cinv.at[2], near_send.at[7], near_recv.at[7], down))

    loads[4].wait()
    loads[5].wait()

    def rates(x, carry):
        mask = inter[x].astype(F32)
        cr[x] = adm[0, x] * mask
        sr[x] = adm[1, x] * mask
        return carry

    lax.fori_loop(0, CX, rates, 0)
    for f in range(4):
        for edge in (0, CX + 1):
            first[f, edge] = jnp.zeros((CY, NZ), F32)
            second[0, f, edge] = jnp.zeros((CY, NZ), F32)
            second[1, f, edge] = jnp.zeros((CY, NZ), F32)

    inside = [
        jnp.where(brick > 0, 1.0, 0.0).astype(F32), jnp.where(brick < 31, 1.0, 0.0).astype(F32),
        jnp.where(grp > 0, 1.0, 0.0).astype(F32), jnp.where(grp < 7, 1.0, 0.0).astype(F32),
    ]
    for copy in (cond_up, cond_down, cond_right, cond_left):
        copy.wait_recv()
    for i in range(2):
        cd[i, 0] = hxc[0, i] * inside[0]
        cd[i, CX + 1] = hxc[1, i] * inside[1]

    def weigh(x, carry):
        out_low = jnp.where((x == 0) & (brick == 0), 1.0, 0.0).astype(F32)
        out_high = jnp.where((x == CX - 1) & (brick == 31), 1.0, 0.0).astype(F32)
        charge = cr[x]
        for i in range(2):
            here = cd[i, x + 1]
            low = 0.5 * (here + cd[i, x])
            high = 0.5 * (here + cd[i, x + 2])
            before = hyc[0, i, pl.ds(x, 1), :] * inside[2]
            after = hyc[1, i, pl.ds(x, 1), :] * inside[3]
            ym = 0.5 * (here + jnp.where(slab_row == 0, before, roll(here, 1, 0)))
            yp = 0.5 * (here + jnp.where(slab_row == CY - 1, after, roll(here, -1, 0)))
            zm = 0.5 * (here + jnp.where(slab_col == 0, 0.0, roll(here, 1, 1)))
            zp = 0.5 * (here + jnp.where(slab_col == NZ - 1, 0.0, roll(here, -1, 1)))
            total = low + high + ym + yp + zm + zp + EPS_SHIFT
            tw[i, x] = total
            dinv[i, x] = 1.0 / (total + charge)
            ee[i, x] = (
                EPS_SHIFT + zm + zp + out_low * low + out_high * high
                + jnp.where(slab_row == 0, ym, 0.0) * (1.0 - inside[2])
                + jnp.where(slab_row == CY - 1, yp, 0.0) * (1.0 - inside[3])
            )
            wx[i, x] = low * (1.0 - out_low)
            wx[i, x + 1] = high * (1.0 - out_high)
            wyb[0, i, pl.ds(x, 1), :] = ym[0:1] * inside[2]
            wyb[1, i, pl.ds(x, 1), :] = yp[CY - 1 : CY] * inside[3]
            wym[i, x] = jnp.where(slab_row == 0, 0.0, ym)
            wyp[i, x] = jnp.where(slab_row == CY - 1, 0.0, yp)
            wzm[i, x] = jnp.where(slab_col == 0, 0.0, zm)
            wzp[i, x] = jnp.where(slab_col == NZ - 1, 0.0, zp)
        return carry

    ends = lambda n: n + 4 * (n // 2)
    lax.fori_loop(0, 4, lambda n, c: weigh(ends(n), c), 0)

    def around(v, f, x, center):
        i = f // 2
        return (
            wx[i, x] * v[f, x] + wx[i, x + 1] * v[f, x + 2]
            + wym[i, x] * roll(center, 1, 0) + wyp[i, x] * roll(center, -1, 0)
            + wzm[i, x] * roll(center, 1, 1) + wzp[i, x] * roll(center, -1, 1)
        )

    def smooth(given, k, between):
        out = second.at[k % 2]

        def scaled(x, carry):
            for f in range(4):
                first[f, x + 1] = given[f, x] * dinv[f // 2, x]
            return carry

        def stencil(x, carry):
            v = [first[f, x + 1] for f in range(4)]
            real, imag = sr[x] * (v[0] - v[2]), sr[x] * (v[1] - v[3])
            swirl = (imag, -real, -imag, real)
            for f in range(4):
                value = v[f] + dinv[f // 2, x] * (around(first, f, x, v[f]) + cr[x] * v[f ^ 2] + swirl[f])
                out[f, x + 1] = value
                sy[k, 0, f, pl.ds(x, 1), :] = value[0:1]
                sy[k, 1, f, pl.ds(x, 1), :] = value[CY - 1 : CY]
            return carry

        lax.fori_loop(0, 4, lambda n, c: scaled(ends(n), c), 0)
        lax.fori_loop(0, 2, lambda n, c: stencil(n * (CX - 1), c), 0)
        halos = [
            remote(out.at[:, CX], hx.at[k, 0], halo_sem.at[k, 0, 0], halo_sem.at[k, 1, 0], up),
            remote(out.at[:, 1], hx.at[k, 1], halo_sem.at[k, 0, 1], halo_sem.at[k, 1, 1], down),
        ]
        for copy in halos:
            copy.start()
        between()
        lax.fori_loop(2, CX - 2, scaled, 0)
        lax.fori_loop(1, CX - 1, stencil, 0)
        sides = [
            remote(sy.at[k, 1], hy.at[k, 0], halo_sem.at[k, 0, 2], halo_sem.at[k, 1, 2], right),
            remote(sy.at[k, 0], hy.at[k, 1], halo_sem.at[k, 0, 3], halo_sem.at[k, 1, 3], left),
        ]
        for copy in sides:
            copy.start()
        return halos + sides

    def operate(k):
        v = second.at[k % 2]

        def stencil(x, carry):
            c = [v[f, x + 1] for f in range(4)]
            over_real, over_imag = c[0] - c[2], c[1] - c[3]
            real = cr[x] * over_real - sr[x] * over_imag
            imag = cr[x] * over_imag + sr[x] * over_real
            flow = (real, imag, -real, -imag)
            for f in range(4):
                u[f, x] = tw[f // 2, x] * c[f] - around(v, f, x, c[f]) + flow[f]
            return carry

        lax.fori_loop(0, CX, stencil, 0)

    def receive_halos(k, copies):
        for copy in copies:
            copy.wait_recv()
        for f in range(4):
            u[f, 0] = u[f, 0] - wx[f // 2, 0] * hx[k, 0, f]
            u[f, CX - 1] = u[f, CX - 1] - wx[f // 2, CX] * hx[k, 1, f]

        def rows(x, carry):
            for f in range(4):
                for side, y in ((0, 0), (1, CY - 1)):
                    u[f, x, y : y + 1, :] = u[f, x, y : y + 1, :] - (
                        wyb[side, f // 2, pl.ds(x, 1), :] * hy[k, side, f, pl.ds(x, 1), :]
                    )
            return carry

        lax.fori_loop(0, CX, rows, 0)
        for copy in copies:
            copy.wait_send()

    def correct(coarse):
        profile = []
        for j in range(3):
            per_field = []
            for f in range(4):
                product = jnp.zeros((8, LANES), F32)
                for s in range(8):
                    product = product + cinv[j, 8 * f : 8 * f + 8, LANES * s : LANES * s + LANES] * coarse[s]
                value = jnp.sum(product, axis=1, keepdims=True)
                per_field.append(jnp.sum(value * onehot[j], axis=0, keepdims=True))
            profile.append(per_field)
        own = profile[1]
        rows = own + [roll(own[f], 1, 1) for f in range(4)] + [roll(own[f], -1, 1) for f in range(4)]
        rows = rows + [own[0] - own[2], own[1] - own[3]]
        for n, value in enumerate(rows):
            table[n] = jnp.broadcast_to(value, (8, NZ))
        for f in range(4):
            u[f, 0] = u[f, 0] - wx[f // 2, 0] * (profile[0][f] - own[f])
            u[f, CX - 1] = u[f, CX - 1] - wx[f // 2, CX] * (profile[2][f] - own[f])

    def advance(k, alpha):
        zero = jnp.zeros((8, LANES), F32)
        ri, ii = zero, zero
        planes = [[] for _ in range(4)]
        for t in range(TILES):
            lanes = slice(LANES * t, LANES * (t + 1))
            p = [table[n, :, lanes] for n in range(14)]

            def step(x, carry):
                ri, ii, *sums = carry
                for half in range(2):
                    at = (x, slice(8 * half, 8 * half + 8), lanes)
                    charge, storage = cr[at], sr[at]
                    real = charge * p[12] - storage * p[13]
                    imag = charge * p[13] + storage * p[12]
                    flow = (real, imag, -real, -imag)
                    for f in range(4):
                        i = f // 2
                        raised = u[(f,) + at] + (
                            ee[(i,) + at] * p[f] - wzm[(i,) + at] * p[4 + f] - wzp[(i,) + at] * p[8 + f] + flow[f]
                        )
                        left_over = r[(f,) + at]
                        if k > 0:
                            old = q[(f,) + at]
                            left_over = left_over - alpha * old
                            r[(f,) + at] = left_over
                            raised = old - alpha * raised
                        q[(f,) + at] = raised
                        ri = ri + left_over * raised
                        ii = ii + raised * raised
                        sums[f] = sums[f] + raised
                return (ri, ii, *sums)

            ri, ii, *sums = lax.fori_loop(0, CX, step, (ri, ii, zero, zero, zero, zero))
            for f in range(4):
                planes[f].append(sums[f])
        return ri, ii, [jnp.concatenate(parts, axis=1) for parts in planes]

    def update_search(k, alpha):
        smoothed = second.at[k % 2]

        def step(x, carry):
            for f in range(4):
                put = smoothed[f, x + 1] + jnp.concatenate([table[f], table[f]], axis=0)
                if k == 0:
                    z[f, x] = put
                else:
                    old = z[f, x]
                    sol[f, x] = alpha * old if k == 1 else sol[f, x] + alpha * old
                    z[f, x] = old - alpha * put
            return carry

        lax.fori_loop(0, CX, step, 0)

    slot = (cz % 4) * 32 + cx * 8 + cy * 2 + cz // 4
    sibling = {"brick": brick, "grp": cx * 2 + 1 - core}

    def share(k, ri, ii, planes):
        coarse = restrict_row(planes, 0)
        ri = jnp.sum(jnp.sum(ri, axis=0, keepdims=True), axis=1, keepdims=True)
        ii = jnp.sum(jnp.sum(ii, axis=0, keepdims=True), axis=1, keepdims=True)
        row_c[k] = jnp.where(lane[0:1] < 32, coarse, jnp.where(lane[0:1] < 64, ri, ii))
        copy = remote(row_c.at[k], slots_c.at[k], core_sem.at[k, 0], core_sem.at[k, 1], sibling)
        copy.start()
        copy.wait_recv()
        row_all[k] = row_c[k] + slots_c[k]

        def send(by, bx):
            remote(
                row_all.at[k], slots_all.at[k, pl.ds(slot, 1)], all_send.at[k], all_recv.at[k],
                {"brick": by, "grp": bx},
            ).start()

        def far(n, carry):
            half = (n + 1) // 2
            dz = 4 + half * (1 - 2 * (n % 2))
            bz = (cz + dz) % 8
            for dy, dx in far_first:
                send(ys[dy] + bz, xs[dx] + core)
            return carry

        lax.fori_loop(0, 7, far, 0)
        for dy, dx in far_first[:-1]:
            send(ys[dy] + cz, xs[dx] + core)
        pltpu.make_async_copy(
            row_all.at[k], slots_all.at[k, pl.ds(slot, 1)], all_recv.at[k]
        ).start()
        return copy

    def gather(k):
        await_bytes(slots_all.at[k], all_recv.at[k])
        quarters = []
        for n in range(4):
            rows = slots_all[k, 32 * n : 32 * n + 8]
            for m in range(1, 4):
                rows = rows + slots_all[k, 32 * n + 8 * m : 32 * n + 8 * m + 8]
            quarters.append(rows)
        dots = jnp.sum(quarters[0] + quarters[1] + quarters[2] + quarters[3], axis=0, keepdims=True)
        alpha = (roll(dots, 64, 1) / (dots + 1e-6))[:, LANES - 1 :]
        quarters = [jnp.where(lane < 32, rows, 0.0) for rows in quarters]
        rows = quarters[0] + roll(quarters[1], 32, 1) + roll(quarters[2], 64, 1) + roll(quarters[3], 96, 1)
        return [rows[s : s + 1] for s in range(8)], jnp.broadcast_to(alpha, (1, LANES))

    def pass_on():
        await_bytes(slots_z, p0_recv.at[0])
        row_p[0] = jnp.sum(slots_z[0:4], axis=0, keepdims=True)
        row_p[1] = jnp.sum(slots_z[4:8], axis=0, keepdims=True)
        mine = slots_p.at[pl.ds(2 * cy, 2), pl.ds(grp, 1)]
        for dev in plane:
            remote(row_p, mine, p0_send.at[1], p0_recv.at[1], dev).start()
        pltpu.make_async_copy(row_p, mine, p0_recv.at[1]).start()
        lax.fori_loop(2, CX - 2, weigh, 0)

    halos = smooth(r, 0, pass_on)
    operate(0)
    receive_halos(0, halos)
    for copy in (hot_up, hot_down, cinv_up, cinv_down):
        copy.wait_recv()
    await_bytes(slots_p, p0_recv.at[1])
    coarse = [jnp.sum(slots_p[s], axis=0, keepdims=True) for s in range(8)]
    alpha = None
    cores = []
    for k in range(ITERS):
        correct(coarse)
        ri, ii, planes = advance(k, None if k == 0 else jnp.broadcast_to(alpha, (8, LANES)))
        cores.append(share(k, ri, ii, planes))
        wide = None if k == 0 else jnp.broadcast_to(jnp.concatenate([alpha] * TILES, axis=1), (CY, NZ))
        if k < ITERS - 1:
            halos = smooth(q, k + 1, lambda: None)
        update_search(k, wide)
        if k < ITERS - 1:
            operate(k + 1)
            receive_halos(k + 1, halos)
        coarse, alpha = gather(k)

    wide = jnp.broadcast_to(jnp.concatenate([alpha] * TILES, axis=1), (CY, NZ))

    def finish(x, carry):
        for f in range(4):
            sol_h[f, x] = sol[f, x] + wide * z[f, x]
            res_h[f, x] = r[f, x] - wide * q[f, x]
        return carry

    lax.fori_loop(0, CX, finish, 0)
    outs = []
    for copy in outs:
        copy.start()
    for copy in started + cores:
        copy.wait_send()
    await_bytes(sizes.at[pl.ds(0, 7)], p0_send.at[0])
    await_bytes(sizes.at[pl.ds(0, 62)], p0_send.at[1])
    for k in range(ITERS):
        await_bytes(sizes, all_send.at[k])
    for copy in outs:
        copy.wait()


def local(source, phase_label, interface, conductivity, admittance, extents, coarse_inverse):
    block = (CX, CY, NZ)
    padded = (CX + 2, CY, NZ)
    vmem = lambda *shape: pltpu.VMEM(shape, F32)
    ints = pltpu.VMEM(block, jnp.int32)
    dma = lambda *shape: pltpu.SemaphoreType.DMA(shape)
    scratch = [
        vmem(4, *block), vmem(4, *block), vmem(4, *block), vmem(4, *block), vmem(4, *block),
        vmem(4, *padded), vmem(2, 4, *padded), vmem(2, *block), ints, ints, vmem(2, *block),
        vmem(2, *padded), vmem(*block), vmem(*block),
        vmem(2, CX + 1, CY, NZ), vmem(2, *block), vmem(2, *block), vmem(2, *block), vmem(2, *block),
        vmem(2, *block), vmem(2, *block), vmem(2, *block), vmem(2, 2, CX, NZ),
        vmem(3, 4 * KB, 1024), vmem(3, KB, NZ), vmem(14, 8, NZ),
        vmem(2, 2, CY, NZ), vmem(2, 2, CX, NZ), vmem(2, 2, CX, NZ),
        vmem(3, 2, 4, CY, NZ), vmem(3, 2, 4, CX, NZ), vmem(3, 2, 4, CX, NZ),
        vmem(1, LANES), vmem(8, LANES), vmem(2, 1, LANES), vmem(8, 8, LANES),
        vmem(3, 1, LANES), vmem(3, 1, LANES), vmem(3, 1, LANES), vmem(3, 128, LANES), vmem(127, 1, LANES),
        dma(6), dma(2), dma(8), dma(8), dma(1), dma(3, 2, 4), dma(3), dma(3), dma(3, 2), dma(3), dma(3),
    ]
    hbm = pl.BlockSpec(memory_space=pl.ANY)
    out = pltpu.VMEM((4, *block), F32)
    return pl.pallas_call(
        kernel,
        out_shape=(out, out),
        in_specs=[pl.BlockSpec(memory_space=pltpu.SMEM)] + [hbm] * 6,
        out_specs=(pl.BlockSpec(memory_space=pltpu.VMEM),)*2,
        scratch_shapes=scratch,
        compiler_params=pltpu.CompilerParams(
            collective_id=0, has_side_effects=True, vmem_limit_bytes=60 * 1024 * 1024
        ),
    )(extents, source, phase_label, interface, conductivity, admittance, coarse_inverse)


def solution(mesh):
    placed = (
        P(None, "brick", "grp", None),
        P("brick", "grp", None),
        P("brick", "grp", None),
        P(None, "brick", "grp", None),
        P(None, "brick", "grp", None),
        P("brick", None),
        P("brick", None),
    )
    return jax.shard_map(
        local,
        mesh=mesh,
        in_specs=placed,
        out_specs=(P(None, "brick", "grp", None), P(None, "brick", "grp", None)),
        check_vma=False,
    )
```

```python
import jax
import jax.numpy as jnp
from jax import lax
from jax.experimental import pallas as pl
from jax.experimental.pallas import tpu as pltpu
from jax.sharding import PartitionSpec as P

CX, CY, NZ, KB = 8, 16, 512, 8
ITERS = 3
SLAB_CELLS = 65536.0
EPS_SHIFT = 0.2
LOW_COND = 0.02
LANES = 128
TILES = NZ // LANES
MESH = pl.DeviceIdType.MESH
F32 = jnp.float32


def roll(v, shift, axis):
    return pltpu.roll(v, shift % v.shape[axis], axis)


def kernel(
    ext_h, src_h, phase_h, inter_h, cond_h, adm_h, cinv_h, sol_h, res_h,
    r, q, u, z, sol, first, second, cond, phase, inter, adm, cd, cr, sr,
    wx, wym, wyp, wzm, wzp, tw, ee, dinv, wyb, cinv, onehot, table,
    hxc, hyc, syc, hx, hy, sy, row_z, slots_z, row_p, slots_p, row_c, slots_c, row_all, slots_all, sizes, ext,
    load_sem, out_sem, near_send, near_recv, c_sem, halo_sem, p0_send, p0_recv, core_sem, all_send, all_recv,
):
    brick, grp = lax.axis_index("brick"), lax.axis_index("grp")
    cy, cz, cx, core = brick // 8, brick % 8, grp // 2, grp % 2
    up = {"brick": (brick + 1) % 32, "grp": grp}
    down = {"brick": (brick + 31) % 32, "grp": grp}
    right = {"brick": brick, "grp": (grp + 1) % 8}
    left = {"brick": brick, "grp": (grp + 7) % 8}
    ys = [((cy + j) % 4) * 8 for j in range(4)]
    xs = [((cx + j) % 4) * 2 for j in range(4)]
    far_first = [(dy, dx) for dy in (2, 1, 3, 0) for dx in (2, 1, 3, 0)]
    far_first.sort(key=lambda p: -min(p[0], 4 - p[0]) - min(p[1], 4 - p[1]))
    plane = [
        {"brick": ys[dy] + cz, "grp": xs[dx] + (core if same else 1 - core)}
        for dy, dx in far_first for same in (0, 1) if (dy, dx, same) != (0, 0, 1)
    ]
    along_z = [{"brick": cy * 8 + (cz + j) % 8, "grp": grp} for j in (4, 3, 5, 2, 6, 1, 7)]

    def load(n, a, b):
        return pltpu.make_async_copy(a, b, load_sem.at[n])

    loads = [
        load(0, cond_h, cond), load(1, phase_h, phase), load(2, src_h, r),
        load(3, cinv_h, cinv.at[1]), load(4, inter_h, inter), load(5, adm_h, adm), load(6, ext_h, ext),
    ]
    barrier = pltpu.get_barrier_semaphore()
    greeted = along_z + plane + [up, down]
    for dev in greeted:
        pl.semaphore_signal(barrier, inc=1, device_id=dev, device_id_type=MESH)
    for copy in loads:
        copy.start()

    lane = lax.broadcasted_iota(jnp.int32, (8, LANES), 1)
    sub = lax.broadcasted_iota(jnp.int32, (8, LANES), 0)
    slab_row = lax.broadcasted_iota(jnp.int32, (CY, NZ), 0)
    slab_col = lax.broadcasted_iota(jnp.int32, (CY, NZ), 1)
    base = (cz % 4) * 32

    def remote(a, b, send, recv, dev):
        return pltpu.make_async_remote_copy(
            src_ref=a, dst_ref=b, send_sem=send, recv_sem=recv, device_id=dev, device_id_type=MESH
        )

    def await_bytes(ref, sem):
        pltpu.make_async_copy(ref, ref, sem).wait()

    loads[6].wait()
    depth = lax.broadcasted_iota(jnp.int32, (KB, NZ), 1)
    length = jnp.broadcast_to(ext[...], (KB, KB)).astype(F32)
    earlier = lax.broadcasted_iota(jnp.int32, (KB, KB), 1) < lax.broadcasted_iota(jnp.int32, (KB, KB), 0)
    not_later = lax.broadcasted_iota(jnp.int32, (KB, KB), 1) <= lax.broadcasted_iota(jnp.int32, (KB, KB), 0)
    begins = jnp.sum(jnp.where(earlier, length, 0.0), axis=1, keepdims=True)
    ends = jnp.sum(jnp.where(not_later, length, 0.0), axis=1, keepdims=True)
    depth = depth.astype(F32)
    own_onehot = jnp.where((depth >= begins) & (depth < ends), 1.0, 0.0).astype(F32)
    onehot[1] = own_onehot

    def restrict_row(planes, base):
        spread = jnp.zeros((8, LANES), F32)
        for f in range(4):
            total = jnp.sum(planes[f], axis=0, keepdims=True)
            value = jnp.sum(total * onehot[1], axis=1, keepdims=True)
            spread = spread + jnp.where(lane == base + 8 * f + sub, value, 0.0)
        return jnp.sum(spread, axis=0, keepdims=True) * (1.0 / SLAB_CELLS)

    loads[0].wait()
    loads[1].wait()

    def masked(x, carry):
        for i in range(2):
            value = cond[i, x] * jnp.where(phase[x] == i + 1, 1.0, LOW_COND)
            cd[i, x + 1] = value
            syc[0, i, pl.ds(x, 1), :] = value[0:1]
            syc[1, i, pl.ds(x, 1), :] = value[CY - 1 : CY]
        return carry

    lax.fori_loop(0, CX, masked, 0)

    loads[2].wait()

    def plane_of(x, carry):
        return tuple(carry[f] + r[f, x, 0:8] + r[f, x, 8:16] for f in range(4))

    planes = lax.fori_loop(0, CX, plane_of, tuple(jnp.zeros((8, NZ), F32) for _ in range(4)))
    row_z[...] = restrict_row(planes, base)
    loads[3].wait()

    pl.semaphore_wait(barrier, len(greeted))

    started = []

    def go(copy):
        copy.start()
        started.append(copy)
        return copy

    for dev in along_z:
        remote(row_z, slots_z.at[pl.ds(cz, 1)], p0_send.at[0], p0_recv.at[0], dev).start()
    pltpu.make_async_copy(row_z, slots_z.at[pl.ds(cz, 1)], p0_recv.at[0]).start()
    cond_up = go(remote(cd.at[:, CX], hxc.at[0], near_send.at[0], near_recv.at[0], up))
    cond_down = go(remote(cd.at[:, 1], hxc.at[1], near_send.at[1], near_recv.at[1], down))
    cond_right = go(remote(syc.at[1], hyc.at[0], near_send.at[2], near_recv.at[2], right))
    cond_left = go(remote(syc.at[0], hyc.at[1], near_send.at[3], near_recv.at[3], left))
    hot_up = go(remote(onehot.at[1], onehot.at[0], near_send.at[4], near_recv.at[4], up))
    hot_down = go(remote(onehot.at[1], onehot.at[2], near_send.at[5], near_recv.at[5], down))
    cinv_up = go(remote(cinv.at[1], cinv.at[0], near_send.at[6], near_recv.at[6], up))
    cinv_down = go(remote(cinv.at[1], cinv.at[2], near_send.at[7], near_recv.at[7], down))

    loads[4].wait()
    loads[5].wait()

    def rates(x, carry):
        mask = inter[x].astype(F32)
        cr[x] = adm[0, x] * mask
        sr[x] = adm[1, x] * mask
        return carry

    lax.fori_loop(0, CX, rates, 0)
    for f in range(4):
        for edge in (0, CX + 1):
            first[f, edge] = jnp.zeros((CY, NZ), F32)
            second[0, f, edge] = jnp.zeros((CY, NZ), F32)
            second[1, f, edge] = jnp.zeros((CY, NZ), F32)

    inside = [
        jnp.where(brick > 0, 1.0, 0.0).astype(F32), jnp.where(brick < 31, 1.0, 0.0).astype(F32),
        jnp.where(grp > 0, 1.0, 0.0).astype(F32), jnp.where(grp < 7, 1.0, 0.0).astype(F32),
    ]
    for copy in (cond_up, cond_down, cond_right, cond_left):
        copy.wait_recv()
    for i in range(2):
        cd[i, 0] = hxc[0, i] * inside[0]
        cd[i, CX + 1] = hxc[1, i] * inside[1]

    def weigh(x, carry):
        out_low = jnp.where((x == 0) & (brick == 0), 1.0, 0.0).astype(F32)
        out_high = jnp.where((x == CX - 1) & (brick == 31), 1.0, 0.0).astype(F32)
        charge = cr[x]
        for i in range(2):
            here = cd[i, x + 1]
            low = 0.5 * (here + cd[i, x])
            high = 0.5 * (here + cd[i, x + 2])
            before = hyc[0, i, pl.ds(x, 1), :] * inside[2]
            after = hyc[1, i, pl.ds(x, 1), :] * inside[3]
            ym = 0.5 * (here + jnp.where(slab_row == 0, before, roll(here, 1, 0)))
            yp = 0.5 * (here + jnp.where(slab_row == CY - 1, after, roll(here, -1, 0)))
            zm = 0.5 * (here + jnp.where(slab_col == 0, 0.0, roll(here, 1, 1)))
            zp = 0.5 * (here + jnp.where(slab_col == NZ - 1, 0.0, roll(here, -1, 1)))
            total = low + high + ym + yp + zm + zp + EPS_SHIFT
            tw[i, x] = total
            dinv[i, x] = 1.0 / (total + charge)
            ee[i, x] = (
                EPS_SHIFT + zm + zp + out_low * low + out_high * high
                + jnp.where(slab_row == 0, ym, 0.0) * (1.0 - inside[2])
                + jnp.where(slab_row == CY - 1, yp, 0.0) * (1.0 - inside[3])
            )
            wx[i, x] = low * (1.0 - out_low)
            wx[i, x + 1] = high * (1.0 - out_high)
            wyb[0, i, pl.ds(x, 1), :] = ym[0:1] * inside[2]
            wyb[1, i, pl.ds(x, 1), :] = yp[CY - 1 : CY] * inside[3]
            wym[i, x] = jnp.where(slab_row == 0, 0.0, ym)
            wyp[i, x] = jnp.where(slab_row == CY - 1, 0.0, yp)
            wzm[i, x] = jnp.where(slab_col == 0, 0.0, zm)
            wzp[i, x] = jnp.where(slab_col == NZ - 1, 0.0, zp)
        return carry

    ends = lambda n: n + 4 * (n // 2)
    lax.fori_loop(0, 4, lambda n, c: weigh(ends(n), c), 0)

    def around(v, f, x, center):
        i = f // 2
        return (
            wx[i, x] * v[f, x] + wx[i, x + 1] * v[f, x + 2]
            + wym[i, x] * roll(center, 1, 0) + wyp[i, x] * roll(center, -1, 0)
            + wzm[i, x] * roll(center, 1, 1) + wzp[i, x] * roll(center, -1, 1)
        )

    def smoother(given, k):
        out = second.at[k % 2]

        def scaled(x, carry):
            for f in range(4):
                first[f, x + 1] = given[f, x] * dinv[f // 2, x]
            return carry

        def stencil(x, carry):
            v = [first[f, x + 1] for f in range(4)]
            real, imag = sr[x] * (v[0] - v[2]), sr[x] * (v[1] - v[3])
            swirl = (imag, -real, -imag, real)
            for f in range(4):
                value = v[f] + dinv[f // 2, x] * (around(first, f, x, v[f]) + cr[x] * v[f ^ 2] + swirl[f])
                out[f, x + 1] = value
                sy[k, 0, f, pl.ds(x, 1), :] = value[0:1]
                sy[k, 1, f, pl.ds(x, 1), :] = value[CY - 1 : CY]
            return carry

        halos = [
            remote(out.at[:, CX], hx.at[k, 0], halo_sem.at[k, 0, 0], halo_sem.at[k, 1, 0], up),
            remote(out.at[:, 1], hx.at[k, 1], halo_sem.at[k, 0, 1], halo_sem.at[k, 1, 1], down),
        ]
        sides = [
            remote(sy.at[k, 1], hy.at[k, 0], halo_sem.at[k, 0, 2], halo_sem.at[k, 1, 2], right),
            remote(sy.at[k, 0], hy.at[k, 1], halo_sem.at[k, 0, 3], halo_sem.at[k, 1, 3], left),
        ]

        def edges():
            lax.fori_loop(0, 4, lambda n, c: scaled(ends(n), c), 0)
            lax.fori_loop(0, 2, lambda n, c: stencil(n * (CX - 1), c), 0)

        def send():
            for copy in halos:
                copy.start()

        def interior():
            lax.fori_loop(2, CX - 2, scaled, 0)
            lax.fori_loop(1, CX - 1, stencil, 0)
            for copy in sides:
                copy.start()
            return halos + sides

        return edges, send, interior

    def operate(k):
        v = second.at[k % 2]

        def stencil(x, carry):
            c = [v[f, x + 1] for f in range(4)]
            over_real, over_imag = c[0] - c[2], c[1] - c[3]
            real = cr[x] * over_real - sr[x] * over_imag
            imag = cr[x] * over_imag + sr[x] * over_real
            flow = (real, imag, -real, -imag)
            for f in range(4):
                u[f, x] = tw[f // 2, x] * c[f] - around(v, f, x, c[f]) + flow[f]
            return carry

        lax.fori_loop(0, CX, stencil, 0)

    def receive_halos(k, copies):
        for copy in copies:
            copy.wait_recv()
        for f in range(4):
            u[f, 0] = u[f, 0] - wx[f // 2, 0] * hx[k, 0, f]
            u[f, CX - 1] = u[f, CX - 1] - wx[f // 2, CX] * hx[k, 1, f]

        def rows(x, carry):
            for f in range(4):
                for side, y in ((0, 0), (1, CY - 1)):
                    u[f, x, y : y + 1, :] = u[f, x, y : y + 1, :] - (
                        wyb[side, f // 2, pl.ds(x, 1), :] * hy[k, side, f, pl.ds(x, 1), :]
                    )
            return carry

        lax.fori_loop(0, CX, rows, 0)
        for copy in copies:
            copy.wait_send()

    def correct(coarse):
        profile = []
        for j in range(3):
            per_field = []
            for f in range(4):
                product = jnp.zeros((8, LANES), F32)
                for s in range(8):
                    product = product + cinv[j, 8 * f : 8 * f + 8, LANES * s : LANES * s + LANES] * coarse[s]
                value = jnp.sum(product, axis=1, keepdims=True)
                per_field.append(jnp.sum(value * onehot[j], axis=0, keepdims=True))
            profile.append(per_field)
        own = profile[1]
        rows = own + [roll(own[f], 1, 1) for f in range(4)] + [roll(own[f], -1, 1) for f in range(4)]
        rows = rows + [own[0] - own[2], own[1] - own[3]]
        for n, value in enumerate(rows):
            table[n] = jnp.broadcast_to(value, (8, NZ))
        for f in range(4):
            u[f, 0] = u[f, 0] - wx[f // 2, 0] * (profile[0][f] - own[f])
            u[f, CX - 1] = u[f, CX - 1] - wx[f // 2, CX] * (profile[2][f] - own[f])

    def advance(k, alpha):
        zero = jnp.zeros((8, LANES), F32)
        ri, ii = zero, zero
        planes = [[] for _ in range(4)]
        for t in range(TILES):
            lanes = slice(LANES * t, LANES * (t + 1))
            p = [table[n, :, lanes] for n in range(14)]

            def step(x, carry):
                ri, ii, *sums = carry
                for half in range(2):
                    at = (x, slice(8 * half, 8 * half + 8), lanes)
                    charge, storage = cr[at], sr[at]
                    real = charge * p[12] - storage * p[13]
                    imag = charge * p[13] + storage * p[12]
                    flow = (real, imag, -real, -imag)
                    for f in range(4):
                        i = f // 2
                        raised = u[(f,) + at] + (
                            ee[(i,) + at] * p[f] - wzm[(i,) + at] * p[4 + f] - wzp[(i,) + at] * p[8 + f] + flow[f]
                        )
                        left_over = r[(f,) + at]
                        if k > 0:
                            old = q[(f,) + at]
                            left_over = left_over - alpha * old
                            r[(f,) + at] = left_over
                            raised = old - alpha * raised
                        q[(f,) + at] = raised
                        ri = ri + left_over * raised
                        ii = ii + raised * raised
                        sums[f] = sums[f] + raised
                return (ri, ii, *sums)

            ri, ii, *sums = lax.fori_loop(0, CX, step, (ri, ii, zero, zero, zero, zero), unroll=2)
            for f in range(4):
                planes[f].append(sums[f])
        return ri, ii, [jnp.concatenate(parts, axis=1) for parts in planes]

    def update_search(k, alpha):
        smoothed = second.at[k % 2]

        def step(x, carry):
            for f in range(4):
                put = smoothed[f, x + 1] + jnp.concatenate([table[f], table[f]], axis=0)
                if k == 0:
                    z[f, x] = put
                else:
                    old = z[f, x]
                    sol[f, x] = alpha * old if k == 1 else sol[f, x] + alpha * old
                    z[f, x] = old - alpha * put
            return carry

        lax.fori_loop(0, CX, step, 0)

    slot = (cz % 4) * 32 + cx * 8 + cy * 2 + cz // 4
    sibling = {"brick": brick, "grp": cx * 2 + 1 - core}

    def share(k, ri, ii, planes, edges, send_halos):
        coarse = restrict_row(planes, 0) if k < ITERS - 1 else jnp.zeros((1, LANES), F32)
        ri = jnp.sum(jnp.sum(ri, axis=0, keepdims=True), axis=1, keepdims=True)
        ii = jnp.sum(jnp.sum(ii, axis=0, keepdims=True), axis=1, keepdims=True)
        row_c[k] = jnp.where(lane[0:1] < 32, coarse, jnp.where(lane[0:1] < 64, ri, ii))
        copy = remote(row_c.at[k], slots_c.at[k], core_sem.at[k, 0], core_sem.at[k, 1], sibling)
        copy.start()
        edges()
        copy.wait_recv()
        row_all[k] = row_c[k] + slots_c[k]

        def send(by, bx):
            remote(
                row_all.at[k], slots_all.at[k, pl.ds(slot, 1)], all_send.at[k], all_recv.at[k],
                {"brick": by, "grp": bx},
            ).start()

        def far(n, carry):
            half = (n + 1) // 2
            dz = 4 + half * (1 - 2 * (n % 2))
            bz = (cz + dz) % 8
            for dy, dx in far_first:
                send(ys[dy] + bz, xs[dx] + core)
            return carry

        lax.fori_loop(0, 7, far, 0)
        for dy, dx in far_first[:-1]:
            send(ys[dy] + cz, xs[dx] + core)
        pltpu.make_async_copy(
            row_all.at[k], slots_all.at[k, pl.ds(slot, 1)], all_recv.at[k]
        ).start()
        send_halos()
        return copy

    def gather(k):
        await_bytes(slots_all.at[k], all_recv.at[k])
        quarters = []
        for n in range(4):
            rows = slots_all[k, 32 * n : 32 * n + 8]
            for m in range(1, 4):
                rows = rows + slots_all[k, 32 * n + 8 * m : 32 * n + 8 * m + 8]
            quarters.append(rows)
        dots = jnp.sum(quarters[0] + quarters[1] + quarters[2] + quarters[3], axis=0, keepdims=True)
        alpha = (roll(dots, 64, 1) / (dots + 1e-6))[:, LANES - 1 :]
        quarters = [jnp.where(lane < 32, rows, 0.0) for rows in quarters]
        rows = quarters[0] + roll(quarters[1], 32, 1) + roll(quarters[2], 64, 1) + roll(quarters[3], 96, 1)
        return [rows[s : s + 1] for s in range(8)], jnp.broadcast_to(alpha, (1, LANES))

    def pass_on():
        await_bytes(slots_z, p0_recv.at[0])
        row_p[0] = jnp.sum(slots_z[0:4], axis=0, keepdims=True)
        row_p[1] = jnp.sum(slots_z[4:8], axis=0, keepdims=True)
        mine = slots_p.at[pl.ds(2 * cy, 2), pl.ds(grp, 1)]
        for dev in plane:
            remote(row_p, mine, p0_send.at[1], p0_recv.at[1], dev).start()
        pltpu.make_async_copy(row_p, mine, p0_recv.at[1]).start()
        lax.fori_loop(2, CX - 2, weigh, 0)

    edges, send_halos, interior = smoother(r, 0)
    edges()
    send_halos()
    pass_on()
    halos = interior()
    operate(0)
    receive_halos(0, halos)
    for copy in (hot_up, hot_down, cinv_up, cinv_down):
        copy.wait_recv()
    await_bytes(slots_p, p0_recv.at[1])
    coarse = [jnp.sum(slots_p[s], axis=0, keepdims=True) for s in range(8)]
    alpha = None
    cores = []
    for k in range(ITERS):
        correct(coarse)
        ri, ii, planes = advance(k, None if k == 0 else jnp.broadcast_to(alpha, (8, LANES)))
        edges, send_halos, interior = smoother(q, k + 1) if k < ITERS - 1 else (lambda: None,) * 3
        cores.append(share(k, ri, ii, planes, edges, send_halos))
        wide = None if k == 0 else jnp.broadcast_to(jnp.concatenate([alpha] * TILES, axis=1), (CY, NZ))
        if k < ITERS - 1:
            halos = interior()
        update_search(k, wide)
        if k < ITERS - 1:
            operate(k + 1)
            receive_halos(k + 1, halos)
        coarse, alpha = gather(k)

    wide = jnp.broadcast_to(jnp.concatenate([alpha] * TILES, axis=1), (CY, NZ))

    def finish(x, carry):
        for f in range(4):
            sol_h[f, x] = sol[f, x] + wide * z[f, x]
            res_h[f, x] = r[f, x] - wide * q[f, x]
        return carry

    lax.fori_loop(0, CX, finish, 0)
    outs = []
    for copy in outs:
        copy.start()
    for copy in started + cores:
        copy.wait_send()
    await_bytes(sizes.at[pl.ds(0, 7)], p0_send.at[0])
    await_bytes(sizes.at[pl.ds(0, 62)], p0_send.at[1])
    for k in range(ITERS):
        await_bytes(sizes, all_send.at[k])
    for copy in outs:
        copy.wait()


def local(source, phase_label, interface, conductivity, admittance, extents, coarse_inverse):
    block = (CX, CY, NZ)
    padded = (CX + 2, CY, NZ)
    vmem = lambda *shape: pltpu.VMEM(shape, F32)
    ints = pltpu.VMEM(block, jnp.int32)
    dma = lambda *shape: pltpu.SemaphoreType.DMA(shape)
    scratch = [
        vmem(4, *block), vmem(4, *block), vmem(4, *block), vmem(4, *block), vmem(4, *block),
        vmem(4, *padded), vmem(2, 4, *padded), vmem(2, *block), ints, ints, vmem(2, *block),
        vmem(2, *padded), vmem(*block), vmem(*block),
        vmem(2, CX + 1, CY, NZ), vmem(2, *block), vmem(2, *block), vmem(2, *block), vmem(2, *block),
        vmem(2, *block), vmem(2, *block), vmem(2, *block), vmem(2, 2, CX, NZ),
        vmem(3, 4 * KB, 1024), vmem(3, KB, NZ), vmem(14, 8, NZ),
        vmem(2, 2, CY, NZ), vmem(2, 2, CX, NZ), vmem(2, 2, CX, NZ),
        vmem(3, 2, 4, CY, NZ), vmem(3, 2, 4, CX, NZ), vmem(3, 2, 4, CX, NZ),
        vmem(1, LANES), vmem(8, LANES), vmem(2, 1, LANES), vmem(8, 8, LANES),
        vmem(3, 1, LANES), vmem(3, 1, LANES), vmem(3, 1, LANES), vmem(3, 128, LANES), vmem(127, 1, LANES),
        pltpu.VMEM((1, KB), jnp.int32),
        dma(7), dma(2), dma(8), dma(8), dma(1), dma(3, 2, 4), dma(3), dma(3), dma(3, 2), dma(3), dma(3),
    ]
    hbm = pl.BlockSpec(memory_space=pl.ANY)
    out = pltpu.VMEM((4, *block), F32)
    return pl.pallas_call(
        kernel,
        out_shape=(out, out),
        in_specs=[hbm] * 7,
        out_specs=(pl.BlockSpec(memory_space=pltpu.VMEM),)*2,
        scratch_shapes=scratch,
        compiler_params=pltpu.CompilerParams(
            collective_id=0, has_side_effects=True, vmem_limit_bytes=60 * 1024 * 1024
        ),
    )(extents, source, phase_label, interface, conductivity, admittance, coarse_inverse)


def solution(mesh):
    placed = (
        P(None, "brick", "grp", None),
        P("brick", "grp", None),
        P("brick", "grp", None),
        P(None, "brick", "grp", None),
        P(None, "brick", "grp", None),
        P("brick", None),
        P("brick", None),
    )
    return jax.shard_map(
        local,
        mesh=mesh,
        in_specs=placed,
        out_specs=(P(None, "brick", "grp", None), P(None, "brick", "grp", None)),
        check_vma=False,
    )
```

```python
import jax
import jax.numpy as jnp
from jax import lax
from jax.experimental import pallas as pl
from jax.experimental.pallas import tpu as pltpu
from jax.sharding import PartitionSpec as P

CX, CY, NZ, KB = 8, 16, 512, 8
ITERS = 3
SLAB_CELLS = 65536.0
EPS_SHIFT = 0.2
LOW_COND = 0.02
LANES = 128
TILES = NZ // LANES
MESH = pl.DeviceIdType.MESH
F32 = jnp.float32


def roll(v, shift, axis):
    return pltpu.roll(v, shift % v.shape[axis], axis)


def kernel(
    ext_h, src_h, phase_h, inter_h, cond_h, adm_h, cinv_h, sol_h, res_h,
    r, q, u, z, sol, first, second, cond, phase, inter, adm, cd, cr, sr,
    wx, wym, wyp, wzm, wzp, tw, ee, dinv, wyb, cinv, onehot, table,
    hxc, hyc, syc, hx, hy, sy, row_z, slots_z, row_p, slots_p, row_c, slots_c, row_all, slots_all, sizes, ext, total,
    load_sem, out_sem, near_send, near_recv, c_sem, halo_sem, p0_send, p0_recv, core_sem, all_send, all_recv,
):
    brick, grp = lax.axis_index("brick"), lax.axis_index("grp")
    cy, cz, cx, core = brick // 8, brick % 8, grp // 2, grp % 2
    up = {"brick": (brick + 1) % 32, "grp": grp}
    down = {"brick": (brick + 31) % 32, "grp": grp}
    right = {"brick": brick, "grp": (grp + 1) % 8}
    left = {"brick": brick, "grp": (grp + 7) % 8}
    ys = [((cy + j) % 4) * 8 for j in range(4)]
    xs = [((cx + j) % 4) * 2 for j in range(4)]
    far_first = [(dy, dx) for dy in (2, 1, 3, 0) for dx in (2, 1, 3, 0)]
    far_first.sort(key=lambda p: -min(p[0], 4 - p[0]) - min(p[1], 4 - p[1]))
    plane = [
        {"brick": ys[dy] + cz, "grp": xs[dx] + (core if same else 1 - core)}
        for dy, dx in far_first for same in (0, 1) if (dy, dx, same) != (0, 0, 1)
    ]
    along_z = [{"brick": cy * 8 + (cz + j) % 8, "grp": grp} for j in (4, 3, 5, 2, 6, 1, 7)]

    def load(n, a, b):
        return pltpu.make_async_copy(a, b, load_sem.at[n])

    loads = [
        load(0, cond_h, cond), load(1, phase_h, phase), load(2, src_h, r),
        load(3, cinv_h, cinv.at[1]), load(4, inter_h, inter), load(5, adm_h, adm), load(6, ext_h, ext),
    ]
    barrier = pltpu.get_barrier_semaphore()
    greeted = along_z + plane + [up, down]
    for dev in greeted:
        pl.semaphore_signal(barrier, inc=1, device_id=dev, device_id_type=MESH)
    for copy in loads:
        copy.start()

    lane = lax.broadcasted_iota(jnp.int32, (8, LANES), 1)
    sub = lax.broadcasted_iota(jnp.int32, (8, LANES), 0)
    slab_row = lax.broadcasted_iota(jnp.int32, (CY, NZ), 0)
    slab_col = lax.broadcasted_iota(jnp.int32, (CY, NZ), 1)
    base = (cz % 4) * 32

    def remote(a, b, send, recv, dev):
        return pltpu.make_async_remote_copy(
            src_ref=a, dst_ref=b, send_sem=send, recv_sem=recv, device_id=dev, device_id_type=MESH
        )

    def await_bytes(ref, sem):
        pltpu.make_async_copy(ref, ref, sem).wait()

    loads[6].wait()
    depth = lax.broadcasted_iota(jnp.int32, (KB, NZ), 1)
    length = jnp.broadcast_to(ext[...], (KB, KB)).astype(F32)
    earlier = lax.broadcasted_iota(jnp.int32, (KB, KB), 1) < lax.broadcasted_iota(jnp.int32, (KB, KB), 0)
    not_later = lax.broadcasted_iota(jnp.int32, (KB, KB), 1) <= lax.broadcasted_iota(jnp.int32, (KB, KB), 0)
    begins = jnp.sum(jnp.where(earlier, length, 0.0), axis=1, keepdims=True)
    ends = jnp.sum(jnp.where(not_later, length, 0.0), axis=1, keepdims=True)
    depth = depth.astype(F32)
    own_onehot = jnp.where((depth >= begins) & (depth < ends), 1.0, 0.0).astype(F32)
    onehot[1] = own_onehot

    def restrict_row(planes, base):
        spread = jnp.zeros((8, LANES), F32)
        for f in range(4):
            total = jnp.sum(planes[f], axis=0, keepdims=True)
            value = jnp.sum(total * onehot[1], axis=1, keepdims=True)
            spread = spread + jnp.where(lane == base + 8 * f + sub, value, 0.0)
        return jnp.sum(spread, axis=0, keepdims=True) * (1.0 / SLAB_CELLS)

    loads[0].wait()
    loads[1].wait()

    def masked(x, carry):
        for i in range(2):
            value = cond[i, x] * jnp.where(phase[x] == i + 1, 1.0, LOW_COND)
            cd[i, x + 1] = value
            syc[0, i, pl.ds(x, 1), :] = value[0:1]
            syc[1, i, pl.ds(x, 1), :] = value[CY - 1 : CY]
        return carry

    lax.fori_loop(0, CX, masked, 0)

    loads[2].wait()

    def plane_of(x, carry):
        return tuple(carry[f] + r[f, x, 0:8] + r[f, x, 8:16] for f in range(4))

    planes = lax.fori_loop(0, CX, plane_of, tuple(jnp.zeros((8, NZ), F32) for _ in range(4)))
    row_z[...] = restrict_row(planes, base)
    loads[3].wait()

    pl.semaphore_wait(barrier, len(greeted))

    started = []

    def go(copy):
        copy.start()
        started.append(copy)
        return copy

    for dev in along_z:
        remote(row_z, slots_z.at[pl.ds(cz, 1)], p0_send.at[0], p0_recv.at[0], dev).start()
    pltpu.make_async_copy(row_z, slots_z.at[pl.ds(cz, 1)], p0_recv.at[0]).start()
    cond_up = go(remote(cd.at[:, CX], hxc.at[0], near_send.at[0], near_recv.at[0], up))
    cond_down = go(remote(cd.at[:, 1], hxc.at[1], near_send.at[1], near_recv.at[1], down))
    cond_right = go(remote(syc.at[1], hyc.at[0], near_send.at[2], near_recv.at[2], right))
    cond_left = go(remote(syc.at[0], hyc.at[1], near_send.at[3], near_recv.at[3], left))
    hot_up = go(remote(onehot.at[1], onehot.at[0], near_send.at[4], near_recv.at[4], up))
    hot_down = go(remote(onehot.at[1], onehot.at[2], near_send.at[5], near_recv.at[5], down))
    cinv_up = go(remote(cinv.at[1], cinv.at[0], near_send.at[6], near_recv.at[6], up))
    cinv_down = go(remote(cinv.at[1], cinv.at[2], near_send.at[7], near_recv.at[7], down))

    loads[4].wait()
    loads[5].wait()

    def rates(x, carry):
        mask = inter[x].astype(F32)
        cr[x] = adm[0, x] * mask
        sr[x] = adm[1, x] * mask
        return carry

    lax.fori_loop(0, CX, rates, 0)
    for f in range(4):
        for edge in (0, CX + 1):
            first[f, edge] = jnp.zeros((CY, NZ), F32)
            second[0, f, edge] = jnp.zeros((CY, NZ), F32)
            second[1, f, edge] = jnp.zeros((CY, NZ), F32)

    inside = [
        jnp.where(brick > 0, 1.0, 0.0).astype(F32), jnp.where(brick < 31, 1.0, 0.0).astype(F32),
        jnp.where(grp > 0, 1.0, 0.0).astype(F32), jnp.where(grp < 7, 1.0, 0.0).astype(F32),
    ]
    for copy in (cond_up, cond_down, cond_right, cond_left):
        copy.wait_recv()
    for i in range(2):
        cd[i, 0] = hxc[0, i] * inside[0]
        cd[i, CX + 1] = hxc[1, i] * inside[1]

    def weigh(x, carry):
        out_low = jnp.where((x == 0) & (brick == 0), 1.0, 0.0).astype(F32)
        out_high = jnp.where((x == CX - 1) & (brick == 31), 1.0, 0.0).astype(F32)
        charge = cr[x]
        for i in range(2):
            here = cd[i, x + 1]
            low = 0.5 * (here + cd[i, x])
            high = 0.5 * (here + cd[i, x + 2])
            before = hyc[0, i, pl.ds(x, 1), :] * inside[2]
            after = hyc[1, i, pl.ds(x, 1), :] * inside[3]
            ym = 0.5 * (here + jnp.where(slab_row == 0, before, roll(here, 1, 0)))
            yp = 0.5 * (here + jnp.where(slab_row == CY - 1, after, roll(here, -1, 0)))
            zm = 0.5 * (here + jnp.where(slab_col == 0, 0.0, roll(here, 1, 1)))
            zp = 0.5 * (here + jnp.where(slab_col == NZ - 1, 0.0, roll(here, -1, 1)))
            total = low + high + ym + yp + zm + zp + EPS_SHIFT
            tw[i, x] = total
            dinv[i, x] = 1.0 / (total + charge)
            ee[i, x] = (
                EPS_SHIFT + zm + zp + out_low * low + out_high * high
                + jnp.where(slab_row == 0, ym, 0.0) * (1.0 - inside[2])
                + jnp.where(slab_row == CY - 1, yp, 0.0) * (1.0 - inside[3])
            )
            wx[i, x] = low * (1.0 - out_low)
            wx[i, x + 1] = high * (1.0 - out_high)
            wyb[0, i, pl.ds(x, 1), :] = ym[0:1] * inside[2]
            wyb[1, i, pl.ds(x, 1), :] = yp[CY - 1 : CY] * inside[3]
            wym[i, x] = jnp.where(slab_row == 0, 0.0, ym)
            wyp[i, x] = jnp.where(slab_row == CY - 1, 0.0, yp)
            wzm[i, x] = jnp.where(slab_col == 0, 0.0, zm)
            wzp[i, x] = jnp.where(slab_col == NZ - 1, 0.0, zp)
        return carry

    ends = lambda n: n + 4 * (n // 2)
    lax.fori_loop(0, 4, lambda n, c: weigh(ends(n), c), 0)

    def around(v, f, x, center):
        i = f // 2
        return (
            wx[i, x] * v[f, x] + wx[i, x + 1] * v[f, x + 2]
            + wym[i, x] * roll(center, 1, 0) + wyp[i, x] * roll(center, -1, 0)
            + wzm[i, x] * roll(center, 1, 1) + wzp[i, x] * roll(center, -1, 1)
        )

    def smoother(given, k):
        out = second.at[k % 2]

        def scaled(x, carry):
            for f in range(4):
                first[f, x + 1] = given[f, x] * dinv[f // 2, x]
            return carry

        def stencil(x, carry):
            v = [first[f, x + 1] for f in range(4)]
            real, imag = sr[x] * (v[0] - v[2]), sr[x] * (v[1] - v[3])
            swirl = (imag, -real, -imag, real)
            for f in range(4):
                value = v[f] + dinv[f // 2, x] * (around(first, f, x, v[f]) + cr[x] * v[f ^ 2] + swirl[f])
                out[f, x + 1] = value
                sy[k, 0, f, pl.ds(x, 1), :] = value[0:1]
                sy[k, 1, f, pl.ds(x, 1), :] = value[CY - 1 : CY]
            return carry

        halos = [
            remote(out.at[:, CX], hx.at[k, 0], halo_sem.at[k, 0, 0], halo_sem.at[k, 1, 0], up),
            remote(out.at[:, 1], hx.at[k, 1], halo_sem.at[k, 0, 1], halo_sem.at[k, 1, 1], down),
        ]
        sides = [
            remote(sy.at[k, 1], hy.at[k, 0], halo_sem.at[k, 0, 2], halo_sem.at[k, 1, 2], right),
            remote(sy.at[k, 0], hy.at[k, 1], halo_sem.at[k, 0, 3], halo_sem.at[k, 1, 3], left),
        ]

        def edges():
            lax.fori_loop(0, 4, lambda n, c: scaled(ends(n), c), 0)
            lax.fori_loop(0, 2, lambda n, c: stencil(n * (CX - 1), c), 0)

        def send():
            for copy in halos:
                copy.start()

        def interior():
            lax.fori_loop(2, CX - 2, scaled, 0)
            lax.fori_loop(1, CX - 1, stencil, 0)
            for copy in sides:
                copy.start()
            return halos + sides

        return edges, send, interior

    def operate(k):
        v = second.at[k % 2]

        def stencil(x, carry):
            c = [v[f, x + 1] for f in range(4)]
            over_real, over_imag = c[0] - c[2], c[1] - c[3]
            real = cr[x] * over_real - sr[x] * over_imag
            imag = cr[x] * over_imag + sr[x] * over_real
            flow = (real, imag, -real, -imag)
            for f in range(4):
                u[f, x] = tw[f // 2, x] * c[f] - around(v, f, x, c[f]) + flow[f]
            return carry

        lax.fori_loop(0, CX, stencil, 0)

    def receive_halos(k, copies):
        for copy in copies[2:]:
            copy.wait_recv()

        def rows(x, carry):
            for f in range(4):
                for side, y in ((0, 0), (1, CY - 1)):
                    u[f, x, y : y + 1, :] = u[f, x, y : y + 1, :] - (
                        wyb[side, f // 2, pl.ds(x, 1), :] * hy[k, side, f, pl.ds(x, 1), :]
                    )
            return carry

        lax.fori_loop(0, CX, rows, 0)
        for copy in copies[:2]:
            copy.wait_recv()
        for f in range(4):
            u[f, 0] = u[f, 0] - wx[f // 2, 0] * hx[k, 0, f]
            u[f, CX - 1] = u[f, CX - 1] - wx[f // 2, CX] * hx[k, 1, f]
        for copy in copies:
            copy.wait_send()

    def correct(coarse):
        profile = []
        for j in range(3):
            per_field = []
            for f in range(4):
                product = jnp.zeros((8, LANES), F32)
                for s in range(8):
                    product = product + cinv[j, 8 * f : 8 * f + 8, LANES * s : LANES * s + LANES] * coarse[s]
                value = jnp.sum(product, axis=1, keepdims=True)
                per_field.append(jnp.sum(value * onehot[j], axis=0, keepdims=True))
            profile.append(per_field)
        own = profile[1]
        rows = own + [roll(own[f], 1, 1) for f in range(4)] + [roll(own[f], -1, 1) for f in range(4)]
        rows = rows + [own[0] - own[2], own[1] - own[3]]
        for n, value in enumerate(rows):
            table[n] = jnp.broadcast_to(value, (8, NZ))
        for f in range(4):
            u[f, 0] = u[f, 0] - wx[f // 2, 0] * (profile[0][f] - own[f])
            u[f, CX - 1] = u[f, CX - 1] - wx[f // 2, CX] * (profile[2][f] - own[f])

    def advance(k, alpha):
        zero = jnp.zeros((8, LANES), F32)

        def tile(t, dots):
            lanes = pl.ds(pl.multiple_of(LANES * t, LANES), LANES)
            p = [table[n, :, lanes] for n in range(14)]

            def step(x, carry):
                ri, ii, *sums = carry
                for half in range(2):
                    at = (x, slice(8 * half, 8 * half + 8), lanes)
                    charge, storage = cr[at], sr[at]
                    real = charge * p[12] - storage * p[13]
                    imag = charge * p[13] + storage * p[12]
                    flow = (real, imag, -real, -imag)
                    for f in range(4):
                        i = f // 2
                        raised = u[(f,) + at] + (
                            ee[(i,) + at] * p[f] - wzm[(i,) + at] * p[4 + f] - wzp[(i,) + at] * p[8 + f] + flow[f]
                        )
                        left_over = r[(f,) + at]
                        if k > 0:
                            old = q[(f,) + at]
                            left_over = left_over - alpha * old
                            r[(f,) + at] = left_over
                            raised = old - alpha * raised
                        q[(f,) + at] = raised
                        ri = ri + left_over * raised
                        ii = ii + raised * raised
                        sums[f] = sums[f] + raised
                return (ri, ii, *sums)

            ri, ii, *sums = lax.fori_loop(0, CX, step, (*dots, zero, zero, zero, zero), unroll=4)
            for f in range(4):
                total[f, :, lanes] = sums[f]
            return ri, ii

        ri, ii = lax.fori_loop(0, TILES, tile, (zero, zero))
        return ri, ii, total

    def update_search(k, alpha):
        smoothed = second.at[k % 2]

        def step(x, carry):
            for f in range(4):
                put = smoothed[f, x + 1] + jnp.concatenate([table[f], table[f]], axis=0)
                if k == 0:
                    z[f, x] = put
                else:
                    old = z[f, x]
                    sol[f, x] = alpha * old if k == 1 else sol[f, x] + alpha * old
                    z[f, x] = old - alpha * put
            return carry

        lax.fori_loop(0, CX, step, 0)

    slot = (cz % 4) * 32 + cx * 8 + cy * 2 + cz // 4
    sibling = {"brick": brick, "grp": cx * 2 + 1 - core}

    def share(k, ri, ii, planes, edges, send_halos):
        coarse = restrict_row(planes, 0) if k < ITERS - 1 else jnp.zeros((1, LANES), F32)
        ri = jnp.sum(jnp.sum(ri, axis=0, keepdims=True), axis=1, keepdims=True)
        ii = jnp.sum(jnp.sum(ii, axis=0, keepdims=True), axis=1, keepdims=True)
        row_c[k] = jnp.where(lane[0:1] < 32, coarse, jnp.where(lane[0:1] < 64, ri, ii))
        copy = remote(row_c.at[k], slots_c.at[k], core_sem.at[k, 0], core_sem.at[k, 1], sibling)
        copy.start()
        edges()
        copy.wait_recv()
        row_all[k] = row_c[k] + slots_c[k]

        def send(by, bx):
            remote(
                row_all.at[k], slots_all.at[k, pl.ds(slot, 1)], all_send.at[k], all_recv.at[k],
                {"brick": by, "grp": bx},
            ).start()

        def far(n, carry):
            half = (n + 1) // 2
            dz = 4 + half * (1 - 2 * (n % 2))
            bz = (cz + dz) % 8
            for dy, dx in far_first:
                send(ys[dy] + bz, xs[dx] + core)
            return carry

        lax.fori_loop(0, 7, far, 0)
        for dy, dx in far_first[:-1]:
            send(ys[dy] + cz, xs[dx] + core)
        pltpu.make_async_copy(
            row_all.at[k], slots_all.at[k, pl.ds(slot, 1)], all_recv.at[k]
        ).start()
        send_halos()
        return copy

    def gather(k):
        await_bytes(slots_all.at[k], all_recv.at[k])
        quarters = []
        for n in range(4):
            rows = slots_all[k, 32 * n : 32 * n + 8]
            for m in range(1, 4):
                rows = rows + slots_all[k, 32 * n + 8 * m : 32 * n + 8 * m + 8]
            quarters.append(rows)
        dots = jnp.sum(quarters[0] + quarters[1] + quarters[2] + quarters[3], axis=0, keepdims=True)
        alpha = (roll(dots, 64, 1) / (dots + 1e-6))[:, LANES - 1 :]
        quarters = [jnp.where(lane < 32, rows, 0.0) for rows in quarters]
        rows = quarters[0] + roll(quarters[1], 32, 1) + roll(quarters[2], 64, 1) + roll(quarters[3], 96, 1)
        return [rows[s : s + 1] for s in range(8)], jnp.broadcast_to(alpha, (1, LANES))

    def pass_on():
        await_bytes(slots_z, p0_recv.at[0])
        row_p[0] = jnp.sum(slots_z[0:4], axis=0, keepdims=True)
        row_p[1] = jnp.sum(slots_z[4:8], axis=0, keepdims=True)
        mine = slots_p.at[pl.ds(2 * cy, 2), pl.ds(grp, 1)]
        for dev in plane:
            remote(row_p, mine, p0_send.at[1], p0_recv.at[1], dev).start()
        pltpu.make_async_copy(row_p, mine, p0_recv.at[1]).start()
        lax.fori_loop(2, CX - 2, weigh, 0)

    edges, send_halos, interior = smoother(r, 0)
    edges()
    send_halos()
    pass_on()
    halos = interior()
    operate(0)
    receive_halos(0, halos)
    for copy in (hot_up, hot_down, cinv_up, cinv_down):
        copy.wait_recv()
    await_bytes(slots_p, p0_recv.at[1])
    coarse = [jnp.sum(slots_p[s], axis=0, keepdims=True) for s in range(8)]
    alpha = None
    cores = []
    for k in range(ITERS):
        correct(coarse)
        ri, ii, planes = advance(k, None if k == 0 else jnp.broadcast_to(alpha, (8, LANES)))
        edges, send_halos, interior = smoother(q, k + 1) if k < ITERS - 1 else (lambda: None,) * 3
        cores.append(share(k, ri, ii, planes, edges, send_halos))
        wide = None if k == 0 else jnp.broadcast_to(jnp.concatenate([alpha] * TILES, axis=1), (CY, NZ))
        if k < ITERS - 1:
            halos = interior()
        update_search(k, wide)
        if k < ITERS - 1:
            operate(k + 1)
            receive_halos(k + 1, halos)
        coarse, alpha = gather(k)

    wide = jnp.broadcast_to(jnp.concatenate([alpha] * TILES, axis=1), (CY, NZ))

    def finish(x, carry):
        for f in range(4):
            sol_h[f, x] = sol[f, x] + wide * z[f, x]
            res_h[f, x] = r[f, x] - wide * q[f, x]
        return carry

    lax.fori_loop(0, CX, finish, 0)
    outs = []
    for copy in outs:
        copy.start()
    for copy in started + cores:
        copy.wait_send()
    await_bytes(sizes.at[pl.ds(0, 7)], p0_send.at[0])
    await_bytes(sizes.at[pl.ds(0, 62)], p0_send.at[1])
    for k in range(ITERS):
        await_bytes(sizes, all_send.at[k])
    for copy in outs:
        copy.wait()


def local(source, phase_label, interface, conductivity, admittance, extents, coarse_inverse):
    block = (CX, CY, NZ)
    padded = (CX + 2, CY, NZ)
    vmem = lambda *shape: pltpu.VMEM(shape, F32)
    ints = pltpu.VMEM(block, jnp.int32)
    dma = lambda *shape: pltpu.SemaphoreType.DMA(shape)
    scratch = [
        vmem(4, *block), vmem(4, *block), vmem(4, *block), vmem(4, *block), vmem(4, *block),
        vmem(4, *padded), vmem(2, 4, *padded), vmem(2, *block), ints, ints, vmem(2, *block),
        vmem(2, *padded), vmem(*block), vmem(*block),
        vmem(2, CX + 1, CY, NZ), vmem(2, *block), vmem(2, *block), vmem(2, *block), vmem(2, *block),
        vmem(2, *block), vmem(2, *block), vmem(2, *block), vmem(2, 2, CX, NZ),
        vmem(3, 4 * KB, 1024), vmem(3, KB, NZ), vmem(14, 8, NZ),
        vmem(2, 2, CY, NZ), vmem(2, 2, CX, NZ), vmem(2, 2, CX, NZ),
        vmem(3, 2, 4, CY, NZ), vmem(3, 2, 4, CX, NZ), vmem(3, 2, 4, CX, NZ),
        vmem(1, LANES), vmem(8, LANES), vmem(2, 1, LANES), vmem(8, 8, LANES),
        vmem(3, 1, LANES), vmem(3, 1, LANES), vmem(3, 1, LANES), vmem(3, 128, LANES), vmem(127, 1, LANES),
        pltpu.VMEM((1, KB), jnp.int32), vmem(4, 8, NZ),
        dma(7), dma(2), dma(8), dma(8), dma(1), dma(3, 2, 4), dma(3), dma(3), dma(3, 2), dma(3), dma(3),
    ]
    hbm = pl.BlockSpec(memory_space=pl.ANY)
    out = pltpu.VMEM((4, *block), F32)
    return pl.pallas_call(
        kernel,
        out_shape=(out, out),
        in_specs=[hbm] * 7,
        out_specs=(pl.BlockSpec(memory_space=pltpu.VMEM),)*2,
        scratch_shapes=scratch,
        compiler_params=pltpu.CompilerParams(
            collective_id=0, has_side_effects=True, vmem_limit_bytes=60 * 1024 * 1024
        ),
    )(extents, source, phase_label, interface, conductivity, admittance, coarse_inverse)


def solution(mesh):
    placed = (
        P(None, "brick", "grp", None),
        P("brick", "grp", None),
        P("brick", "grp", None),
        P(None, "brick", "grp", None),
        P(None, "brick", "grp", None),
        P("brick", None),
        P("brick", None),
    )
    return jax.shard_map(
        local,
        mesh=mesh,
        in_specs=placed,
        out_specs=(P(None, "brick", "grp", None), P(None, "brick", "grp", None)),
        check_vma=False,
    )
```

```python
import jax
import jax.numpy as jnp
from jax import lax
from jax.experimental import pallas as pl
from jax.experimental.pallas import tpu as pltpu
from jax.sharding import PartitionSpec as P

CX, CY, NZ, KB = 8, 16, 512, 8
ITERS = 3
SLAB_CELLS = 65536.0
EPS_SHIFT = 0.2
LOW_COND = 0.02
LANES = 128
TILES = NZ // LANES
MESH = pl.DeviceIdType.MESH
F32 = jnp.float32


def roll(v, shift, axis):
    return pltpu.roll(v, shift % v.shape[axis], axis)


def kernel(
    ext_h, src_h, phase_h, inter_h, cond_h, adm_h, cinv_h, sol_h, res_h,
    r, q, u, z, sol, first, second, cond, phase, inter, adm, cd, cr, sr,
    wx, wym, wyp, wzm, wzp, tw, ee, dinv, wyb, cinv, onehot, table,
    hxc, hyc, syc, hx, hy, sy, row_z, slots_z, row_p, slots_p, row_c, slots_c, row_all, slots_all, sizes, ext, total,
    load_sem, out_sem, near_send, near_recv, c_sem, halo_sem, p0_send, p0_recv, core_sem, all_send, all_recv,
):
    brick, grp = lax.axis_index("brick"), lax.axis_index("grp")
    cy, cz, cx, core = brick // 8, brick % 8, grp // 2, grp % 2
    up = {"brick": (brick + 1) % 32, "grp": grp}
    down = {"brick": (brick + 31) % 32, "grp": grp}
    right = {"brick": brick, "grp": (grp + 1) % 8}
    left = {"brick": brick, "grp": (grp + 7) % 8}
    ys = [((cy + j) % 4) * 8 for j in range(4)]
    xs = [((cx + j) % 4) * 2 for j in range(4)]
    far_first = [(dy, dx) for dy in (2, 1, 3, 0) for dx in (2, 1, 3, 0)]
    far_first.sort(key=lambda p: -min(p[0], 4 - p[0]) - min(p[1], 4 - p[1]))
    plane = [
        {"brick": ys[dy] + cz, "grp": xs[dx] + (core if same else 1 - core)}
        for dy, dx in far_first for same in (0, 1) if (dy, dx, same) != (0, 0, 1)
    ]
    along_z = [{"brick": cy * 8 + (cz + j) % 8, "grp": grp} for j in (4, 3, 5, 2, 6, 1, 7)]

    def load(n, a, b):
        return pltpu.make_async_copy(a, b, load_sem.at[n])

    loads = [
        load(0, cond_h, cond), load(1, phase_h, phase), load(2, src_h, r),
        load(3, cinv_h, cinv.at[1]), load(4, inter_h, inter), load(5, adm_h, adm), load(6, ext_h, ext),
    ]
    barrier = pltpu.get_barrier_semaphore()
    greeted = along_z + plane + [up, down]
    for dev in greeted:
        pl.semaphore_signal(barrier, inc=1, device_id=dev, device_id_type=MESH)
    for copy in loads:
        copy.start()

    lane = lax.broadcasted_iota(jnp.int32, (8, LANES), 1)
    sub = lax.broadcasted_iota(jnp.int32, (8, LANES), 0)
    slab_row = lax.broadcasted_iota(jnp.int32, (CY, NZ), 0)
    slab_col = lax.broadcasted_iota(jnp.int32, (CY, NZ), 1)
    base = (cz % 4) * 32

    def remote(a, b, send, recv, dev):
        return pltpu.make_async_remote_copy(
            src_ref=a, dst_ref=b, send_sem=send, recv_sem=recv, device_id=dev, device_id_type=MESH
        )

    def await_bytes(ref, sem):
        pltpu.make_async_copy(ref, ref, sem).wait()

    loads[6].wait()
    depth = lax.broadcasted_iota(jnp.int32, (KB, NZ), 1)
    length = jnp.broadcast_to(ext[...], (KB, KB)).astype(F32)
    earlier = lax.broadcasted_iota(jnp.int32, (KB, KB), 1) < lax.broadcasted_iota(jnp.int32, (KB, KB), 0)
    not_later = lax.broadcasted_iota(jnp.int32, (KB, KB), 1) <= lax.broadcasted_iota(jnp.int32, (KB, KB), 0)
    begins = jnp.sum(jnp.where(earlier, length, 0.0), axis=1, keepdims=True)
    ends = jnp.sum(jnp.where(not_later, length, 0.0), axis=1, keepdims=True)
    depth = depth.astype(F32)
    own_onehot = jnp.where((depth >= begins) & (depth < ends), 1.0, 0.0).astype(F32)
    onehot[1] = own_onehot

    def restrict_row(planes, base):
        spread = jnp.zeros((8, LANES), F32)
        for f in range(4):
            total = jnp.sum(planes[f], axis=0, keepdims=True)
            value = jnp.sum(total * onehot[1], axis=1, keepdims=True)
            spread = spread + jnp.where(lane == base + 8 * f + sub, value, 0.0)
        return jnp.sum(spread, axis=0, keepdims=True) * (1.0 / SLAB_CELLS)

    loads[0].wait()
    loads[1].wait()

    def masked(x, carry):
        for i in range(2):
            value = cond[i, x] * jnp.where(phase[x] == i + 1, 1.0, LOW_COND)
            cd[i, x + 1] = value
            syc[0, i, pl.ds(x, 1), :] = value[0:1]
            syc[1, i, pl.ds(x, 1), :] = value[CY - 1 : CY]
        return carry

    lax.fori_loop(0, CX, masked, 0)

    loads[2].wait()

    def plane_of(x, carry):
        return tuple(carry[f] + r[f, x, 0:8] + r[f, x, 8:16] for f in range(4))

    planes = lax.fori_loop(0, CX, plane_of, tuple(jnp.zeros((8, NZ), F32) for _ in range(4)))
    row_z[...] = restrict_row(planes, base)
    loads[3].wait()

    pl.semaphore_wait(barrier, len(greeted))

    started = []

    def go(copy):
        copy.start()
        started.append(copy)
        return copy

    for dev in along_z:
        remote(row_z, slots_z.at[pl.ds(cz, 1)], p0_send.at[0], p0_recv.at[0], dev).start()
    pltpu.make_async_copy(row_z, slots_z.at[pl.ds(cz, 1)], p0_recv.at[0]).start()
    cond_up = go(remote(cd.at[:, CX], hxc.at[0], near_send.at[0], near_recv.at[0], up))
    cond_down = go(remote(cd.at[:, 1], hxc.at[1], near_send.at[1], near_recv.at[1], down))
    cond_right = go(remote(syc.at[1], hyc.at[0], near_send.at[2], near_recv.at[2], right))
    cond_left = go(remote(syc.at[0], hyc.at[1], near_send.at[3], near_recv.at[3], left))
    hot_up = go(remote(onehot.at[1], onehot.at[0], near_send.at[4], near_recv.at[4], up))
    hot_down = go(remote(onehot.at[1], onehot.at[2], near_send.at[5], near_recv.at[5], down))
    cinv_up = go(remote(cinv.at[1], cinv.at[0], near_send.at[6], near_recv.at[6], up))
    cinv_down = go(remote(cinv.at[1], cinv.at[2], near_send.at[7], near_recv.at[7], down))

    loads[4].wait()
    loads[5].wait()

    def rates(x, carry):
        mask = inter[x].astype(F32)
        cr[x] = adm[0, x] * mask
        sr[x] = adm[1, x] * mask
        return carry

    lax.fori_loop(0, CX, rates, 0)
    for f in range(4):
        for edge in (0, CX + 1):
            first[f, edge] = jnp.zeros((CY, NZ), F32)
            second[0, f, edge] = jnp.zeros((CY, NZ), F32)
            second[1, f, edge] = jnp.zeros((CY, NZ), F32)

    inside = [
        jnp.where(brick > 0, 1.0, 0.0).astype(F32), jnp.where(brick < 31, 1.0, 0.0).astype(F32),
        jnp.where(grp > 0, 1.0, 0.0).astype(F32), jnp.where(grp < 7, 1.0, 0.0).astype(F32),
    ]
    for copy in (cond_up, cond_down, cond_right, cond_left):
        copy.wait_recv()
    for i in range(2):
        cd[i, 0] = hxc[0, i] * inside[0]
        cd[i, CX + 1] = hxc[1, i] * inside[1]

    def weigh(x, carry):
        out_low = jnp.where((x == 0) & (brick == 0), 1.0, 0.0).astype(F32)
        out_high = jnp.where((x == CX - 1) & (brick == 31), 1.0, 0.0).astype(F32)
        charge = cr[x]
        for i in range(2):
            here = cd[i, x + 1]
            low = 0.5 * (here + cd[i, x])
            high = 0.5 * (here + cd[i, x + 2])
            before = hyc[0, i, pl.ds(x, 1), :] * inside[2]
            after = hyc[1, i, pl.ds(x, 1), :] * inside[3]
            ym = 0.5 * (here + jnp.where(slab_row == 0, before, roll(here, 1, 0)))
            yp = 0.5 * (here + jnp.where(slab_row == CY - 1, after, roll(here, -1, 0)))
            zm = 0.5 * (here + jnp.where(slab_col == 0, 0.0, roll(here, 1, 1)))
            zp = 0.5 * (here + jnp.where(slab_col == NZ - 1, 0.0, roll(here, -1, 1)))
            total = low + high + ym + yp + zm + zp + EPS_SHIFT
            tw[i, x] = total
            dinv[i, x] = 1.0 / (total + charge)
            ee[i, x] = (
                EPS_SHIFT + zm + zp + out_low * low + out_high * high
                + jnp.where(slab_row == 0, ym, 0.0) * (1.0 - inside[2])
                + jnp.where(slab_row == CY - 1, yp, 0.0) * (1.0 - inside[3])
            )
            wx[i, x] = low * (1.0 - out_low)
            wx[i, x + 1] = high * (1.0 - out_high)
            wyb[0, i, pl.ds(x, 1), :] = ym[0:1] * inside[2]
            wyb[1, i, pl.ds(x, 1), :] = yp[CY - 1 : CY] * inside[3]
            wym[i, x] = jnp.where(slab_row == 0, 0.0, ym)
            wyp[i, x] = jnp.where(slab_row == CY - 1, 0.0, yp)
            wzm[i, x] = jnp.where(slab_col == 0, 0.0, zm)
            wzp[i, x] = jnp.where(slab_col == NZ - 1, 0.0, zp)
        return carry

    ends = lambda n: n + 4 * (n // 2)
    lax.fori_loop(0, 4, lambda n, c: weigh(ends(n), c), 0)

    def around(v, f, x, center):
        i = f // 2
        return (
            wx[i, x] * v[f, x] + wx[i, x + 1] * v[f, x + 2]
            + wym[i, x] * roll(center, 1, 0) + wyp[i, x] * roll(center, -1, 0)
            + wzm[i, x] * roll(center, 1, 1) + wzp[i, x] * roll(center, -1, 1)
        )

    def smoother(given, k):
        out = second.at[k % 2]

        def scaled(x, carry):
            for f in range(4):
                first[f, x + 1] = given[f, x] * dinv[f // 2, x]
            return carry

        def stencil(x, carry):
            v = [first[f, x + 1] for f in range(4)]
            real, imag = sr[x] * (v[0] - v[2]), sr[x] * (v[1] - v[3])
            swirl = (imag, -real, -imag, real)
            for f in range(4):
                value = v[f] + dinv[f // 2, x] * (around(first, f, x, v[f]) + cr[x] * v[f ^ 2] + swirl[f])
                out[f, x + 1] = value
                sy[k, 0, f, pl.ds(x, 1), :] = value[0:1]
                sy[k, 1, f, pl.ds(x, 1), :] = value[CY - 1 : CY]
            return carry

        halos = [
            remote(out.at[:, CX], hx.at[k, 0], halo_sem.at[k, 0, 0], halo_sem.at[k, 1, 0], up),
            remote(out.at[:, 1], hx.at[k, 1], halo_sem.at[k, 0, 1], halo_sem.at[k, 1, 1], down),
        ]
        sides = [
            remote(sy.at[k, 1], hy.at[k, 0], halo_sem.at[k, 0, 2], halo_sem.at[k, 1, 2], right),
            remote(sy.at[k, 0], hy.at[k, 1], halo_sem.at[k, 0, 3], halo_sem.at[k, 1, 3], left),
        ]

        def edges():
            lax.fori_loop(0, 4, lambda n, c: scaled(ends(n), c), 0)
            lax.fori_loop(0, 2, lambda n, c: stencil(n * (CX - 1), c), 0)

        def send():
            for copy in halos:
                copy.start()

        def interior():
            lax.fori_loop(2, CX - 2, scaled, 0)
            lax.fori_loop(1, CX - 1, stencil, 0)
            for copy in sides:
                copy.start()
            return halos + sides

        return edges, send, interior

    def operate(k):
        v = second.at[k % 2]

        def stencil(x, carry):
            c = [v[f, x + 1] for f in range(4)]
            over_real, over_imag = c[0] - c[2], c[1] - c[3]
            real = cr[x] * over_real - sr[x] * over_imag
            imag = cr[x] * over_imag + sr[x] * over_real
            flow = (real, imag, -real, -imag)
            for f in range(4):
                u[f, x] = tw[f // 2, x] * c[f] - around(v, f, x, c[f]) + flow[f]
            return carry

        lax.fori_loop(0, CX, stencil, 0)

    def receive_halos(k, copies):
        for copy in copies[2:]:
            copy.wait_recv()

        def rows(x, carry):
            for f in range(4):
                for side, y in ((0, 0), (1, CY - 1)):
                    u[f, x, y : y + 1, :] = u[f, x, y : y + 1, :] - (
                        wyb[side, f // 2, pl.ds(x, 1), :] * hy[k, side, f, pl.ds(x, 1), :]
                    )
            return carry

        lax.fori_loop(0, CX, rows, 0)
        for copy in copies[:2]:
            copy.wait_recv()
        for copy in copies:
            copy.wait_send()

    def correct(k, coarse):
        profile = []
        for j in range(3):
            per_field = []
            for f in range(4):
                product = jnp.zeros((8, LANES), F32)
                for s in range(8):
                    product = product + cinv[j, 8 * f : 8 * f + 8, LANES * s : LANES * s + LANES] * coarse[s]
                value = jnp.sum(product, axis=1, keepdims=True)
                per_field.append(jnp.sum(value * onehot[j], axis=0, keepdims=True))
            profile.append(per_field)
        own = profile[1]
        rows = own + [roll(own[f], 1, 1) for f in range(4)] + [roll(own[f], -1, 1) for f in range(4)]
        rows = rows + [own[0] - own[2], own[1] - own[3]]
        for n, value in enumerate(rows):
            table[n] = jnp.broadcast_to(value, (8, NZ))
        for f in range(4):
            u[f, 0] = u[f, 0] - wx[f // 2, 0] * (hx[k, 0, f] + (profile[0][f] - own[f]))
            u[f, CX - 1] = u[f, CX - 1] - wx[f // 2, CX] * (hx[k, 1, f] + (profile[2][f] - own[f]))

    def advance(k, alpha):
        zero = jnp.zeros((8, LANES), F32)

        def tile(t, dots):
            lanes = pl.ds(pl.multiple_of(LANES * t, LANES), LANES)
            p = [table[n, :, lanes] for n in range(14)]

            def step(x, carry):
                ri, ii, *sums = carry
                for half in range(2):
                    at = (x, slice(8 * half, 8 * half + 8), lanes)
                    charge, storage = cr[at], sr[at]
                    real = charge * p[12] - storage * p[13]
                    imag = charge * p[13] + storage * p[12]
                    flow = (real, imag, -real, -imag)
                    for f in range(4):
                        i = f // 2
                        raised = u[(f,) + at] + (
                            ee[(i,) + at] * p[f] - wzm[(i,) + at] * p[4 + f] - wzp[(i,) + at] * p[8 + f] + flow[f]
                        )
                        left_over = r[(f,) + at]
                        if k > 0:
                            old = q[(f,) + at]
                            left_over = left_over - alpha * old
                            r[(f,) + at] = left_over
                            raised = old - alpha * raised
                        q[(f,) + at] = raised
                        ri = ri + left_over * raised
                        ii = ii + raised * raised
                        sums[f] = sums[f] + raised
                return (ri, ii, *sums)

            ri, ii, *sums = lax.fori_loop(0, CX, step, (*dots, zero, zero, zero, zero), unroll=4)
            for f in range(4):
                total[f, :, lanes] = sums[f]
            return ri, ii

        ri, ii = lax.fori_loop(0, TILES, tile, (zero, zero))
        return ri, ii, total

    def update_search(k, alpha):
        smoothed = second.at[k % 2]

        def step(x, carry):
            for f in range(4):
                put = smoothed[f, x + 1] + jnp.concatenate([table[f], table[f]], axis=0)
                if k == 0:
                    z[f, x] = put
                else:
                    old = z[f, x]
                    sol[f, x] = alpha * old if k == 1 else sol[f, x] + alpha * old
                    z[f, x] = old - alpha * put
            return carry

        lax.fori_loop(0, CX, step, 0)

    slot = (cz % 4) * 32 + cx * 8 + cy * 2 + cz // 4
    sibling = {"brick": brick, "grp": cx * 2 + 1 - core}

    def share(k, ri, ii, planes, edges, send_halos):
        coarse = restrict_row(planes, 0) if k < ITERS - 1 else jnp.zeros((1, LANES), F32)
        ri = jnp.sum(jnp.sum(ri, axis=0, keepdims=True), axis=1, keepdims=True)
        ii = jnp.sum(jnp.sum(ii, axis=0, keepdims=True), axis=1, keepdims=True)
        row_c[k] = jnp.where(lane[0:1] < 32, coarse, jnp.where(lane[0:1] < 64, ri, ii))
        copy = remote(row_c.at[k], slots_c.at[k], core_sem.at[k, 0], core_sem.at[k, 1], sibling)
        copy.start()
        edges()
        copy.wait_recv()
        row_all[k] = row_c[k] + slots_c[k]

        def send(by, bx):
            remote(
                row_all.at[k], slots_all.at[k, pl.ds(slot, 1)], all_send.at[k], all_recv.at[k],
                {"brick": by, "grp": bx},
            ).start()

        def far(n, carry):
            half = (n + 1) // 2
            dz = 4 + half * (1 - 2 * (n % 2))
            bz = (cz + dz) % 8
            for dy, dx in far_first:
                send(ys[dy] + bz, xs[dx] + core)
            return carry

        lax.fori_loop(0, 7, far, 0)
        for dy, dx in far_first[:-1]:
            send(ys[dy] + cz, xs[dx] + core)
        pltpu.make_async_copy(
            row_all.at[k], slots_all.at[k, pl.ds(slot, 1)], all_recv.at[k]
        ).start()
        send_halos()
        return copy

    def gather(k):
        await_bytes(slots_all.at[k], all_recv.at[k])
        quarters = []
        for n in range(4):
            rows = slots_all[k, 32 * n : 32 * n + 8]
            for m in range(1, 4):
                rows = rows + slots_all[k, 32 * n + 8 * m : 32 * n + 8 * m + 8]
            quarters.append(rows)
        dots = jnp.sum(quarters[0] + quarters[1] + quarters[2] + quarters[3], axis=0, keepdims=True)
        alpha = (roll(dots, 64, 1) / (dots + 1e-6))[:, LANES - 1 :]
        quarters = [jnp.where(lane < 32, rows, 0.0) for rows in quarters]
        rows = quarters[0] + roll(quarters[1], 32, 1) + roll(quarters[2], 64, 1) + roll(quarters[3], 96, 1)
        return [rows[s : s + 1] for s in range(8)], jnp.broadcast_to(alpha, (1, LANES))

    def pass_on():
        await_bytes(slots_z, p0_recv.at[0])
        row_p[0] = jnp.sum(slots_z[0:4], axis=0, keepdims=True)
        row_p[1] = jnp.sum(slots_z[4:8], axis=0, keepdims=True)
        mine = slots_p.at[pl.ds(2 * cy, 2), pl.ds(grp, 1)]
        for dev in plane:
            remote(row_p, mine, p0_send.at[1], p0_recv.at[1], dev).start()
        pltpu.make_async_copy(row_p, mine, p0_recv.at[1]).start()
        lax.fori_loop(2, CX - 2, weigh, 0)

    edges, send_halos, interior = smoother(r, 0)
    edges()
    send_halos()
    pass_on()
    halos = interior()
    operate(0)
    receive_halos(0, halos)
    for copy in (hot_up, hot_down, cinv_up, cinv_down):
        copy.wait_recv()
    await_bytes(slots_p, p0_recv.at[1])
    coarse = [jnp.sum(slots_p[s], axis=0, keepdims=True) for s in range(8)]
    alpha = None
    cores = []
    for k in range(ITERS):
        correct(k, coarse)
        ri, ii, planes = advance(k, None if k == 0 else jnp.broadcast_to(alpha, (8, LANES)))
        edges, send_halos, interior = smoother(q, k + 1) if k < ITERS - 1 else (lambda: None,) * 3
        cores.append(share(k, ri, ii, planes, edges, send_halos))
        wide = None if k == 0 else jnp.broadcast_to(jnp.concatenate([alpha] * TILES, axis=1), (CY, NZ))
        if k < ITERS - 1:
            halos = interior()
        update_search(k, wide)
        if k < ITERS - 1:
            operate(k + 1)
            receive_halos(k + 1, halos)
        coarse, alpha = gather(k)

    wide = jnp.broadcast_to(jnp.concatenate([alpha] * TILES, axis=1), (CY, NZ))

    def finish(x, carry):
        for f in range(4):
            sol_h[f, x] = sol[f, x] + wide * z[f, x]
            res_h[f, x] = r[f, x] - wide * q[f, x]
        return carry

    lax.fori_loop(0, CX, finish, 0)
    outs = []
    for copy in outs:
        copy.start()
    for copy in started + cores:
        copy.wait_send()
    await_bytes(sizes.at[pl.ds(0, 7)], p0_send.at[0])
    await_bytes(sizes.at[pl.ds(0, 62)], p0_send.at[1])
    for k in range(ITERS):
        await_bytes(sizes, all_send.at[k])
    for copy in outs:
        copy.wait()


def local(source, phase_label, interface, conductivity, admittance, extents, coarse_inverse):
    block = (CX, CY, NZ)
    padded = (CX + 2, CY, NZ)
    vmem = lambda *shape: pltpu.VMEM(shape, F32)
    ints = pltpu.VMEM(block, jnp.int32)
    dma = lambda *shape: pltpu.SemaphoreType.DMA(shape)
    scratch = [
        vmem(4, *block), vmem(4, *block), vmem(4, *block), vmem(4, *block), vmem(4, *block),
        vmem(4, *padded), vmem(2, 4, *padded), vmem(2, *block), ints, ints, vmem(2, *block),
        vmem(2, *padded), vmem(*block), vmem(*block),
        vmem(2, CX + 1, CY, NZ), vmem(2, *block), vmem(2, *block), vmem(2, *block), vmem(2, *block),
        vmem(2, *block), vmem(2, *block), vmem(2, *block), vmem(2, 2, CX, NZ),
        vmem(3, 4 * KB, 1024), vmem(3, KB, NZ), vmem(14, 8, NZ),
        vmem(2, 2, CY, NZ), vmem(2, 2, CX, NZ), vmem(2, 2, CX, NZ),
        vmem(3, 2, 4, CY, NZ), vmem(3, 2, 4, CX, NZ), vmem(3, 2, 4, CX, NZ),
        vmem(1, LANES), vmem(8, LANES), vmem(2, 1, LANES), vmem(8, 8, LANES),
        vmem(3, 1, LANES), vmem(3, 1, LANES), vmem(3, 1, LANES), vmem(3, 128, LANES), vmem(127, 1, LANES),
        pltpu.VMEM((1, KB), jnp.int32), vmem(4, 8, NZ),
        dma(7), dma(2), dma(8), dma(8), dma(1), dma(3, 2, 4), dma(3), dma(3), dma(3, 2), dma(3), dma(3),
    ]
    hbm = pl.BlockSpec(memory_space=pl.ANY)
    out = pltpu.VMEM((4, *block), F32)
    return pl.pallas_call(
        kernel,
        out_shape=(out, out),
        in_specs=[hbm] * 7,
        out_specs=(pl.BlockSpec(memory_space=pltpu.VMEM),)*2,
        scratch_shapes=scratch,
        compiler_params=pltpu.CompilerParams(
            collective_id=0, has_side_effects=True, vmem_limit_bytes=60 * 1024 * 1024
        ),
    )(extents, source, phase_label, interface, conductivity, admittance, coarse_inverse)


def solution(mesh):
    placed = (
        P(None, "brick", "grp", None),
        P("brick", "grp", None),
        P("brick", "grp", None),
        P(None, "brick", "grp", None),
        P(None, "brick", "grp", None),
        P("brick", None),
        P("brick", None),
    )
    return jax.shard_map(
        local,
        mesh=mesh,
        in_specs=placed,
        out_specs=(P(None, "brick", "grp", None), P(None, "brick", "grp", None)),
        check_vma=False,
    )
```

```python
import jax
import jax.numpy as jnp
from jax import lax
from jax.experimental import pallas as pl
from jax.experimental.pallas import tpu as pltpu
from jax.sharding import PartitionSpec as P

CX, CY, NZ, KB = 8, 16, 512, 8
ITERS = 3
SLAB_CELLS = 65536.0
EPS_SHIFT = 0.2
LOW_COND = 0.02
LANES = 128
TILES = NZ // LANES
MESH = pl.DeviceIdType.MESH
F32 = jnp.float32


def roll(v, shift, axis):
    return pltpu.roll(v, shift % v.shape[axis], axis)


def kernel(
    ext_h, src_h, phase_h, inter_h, cond_h, adm_h, cinv_h, sol, z, r, q, last_alpha,
    u, first, second, cond, phase, inter, adm, cd, cr, sr,
    wx, wym, wyp, wzm, wzp, tw, ee, dinv, wyb, cinv, onehot, table,
    hxc, hyc, syc, hx, hy, sy, row_z, slots_z, row_p, slots_p, row_c, slots_c, row_all, slots_all, sizes, ext, total,
    load_sem, near_send, near_recv, c_sem, halo_sem, p0_send, p0_recv, core_sem, all_send, all_recv,
):
    brick, grp = lax.axis_index("brick"), lax.axis_index("grp")
    cy, cz, cx, core = brick // 8, brick % 8, grp // 2, grp % 2
    up = {"brick": (brick + 1) % 32, "grp": grp}
    down = {"brick": (brick + 31) % 32, "grp": grp}
    right = {"brick": brick, "grp": (grp + 1) % 8}
    left = {"brick": brick, "grp": (grp + 7) % 8}
    ys = [((cy + j) % 4) * 8 for j in range(4)]
    xs = [((cx + j) % 4) * 2 for j in range(4)]
    far_first = [(dy, dx) for dy in (2, 1, 3, 0) for dx in (2, 1, 3, 0)]
    far_first.sort(key=lambda p: -min(p[0], 4 - p[0]) - min(p[1], 4 - p[1]))
    plane = [
        {"brick": ys[dy] + cz, "grp": xs[dx] + (core if same else 1 - core)}
        for dy, dx in far_first for same in (0, 1) if (dy, dx, same) != (0, 0, 1)
    ]
    along_z = [{"brick": cy * 8 + (cz + j) % 8, "grp": grp} for j in (4, 3, 5, 2, 6, 1, 7)]

    def load(n, a, b):
        return pltpu.make_async_copy(a, b, load_sem.at[n])

    loads = [
        load(0, cond_h, cond), load(1, phase_h, phase), load(2, src_h, r),
        load(3, cinv_h, cinv.at[1]), load(4, inter_h, inter), load(5, adm_h, adm), load(6, ext_h, ext),
    ]
    barrier = pltpu.get_barrier_semaphore()
    greeted = along_z + plane + [up, down]
    for dev in greeted:
        pl.semaphore_signal(barrier, inc=1, device_id=dev, device_id_type=MESH)
    for copy in loads:
        copy.start()

    lane = lax.broadcasted_iota(jnp.int32, (8, LANES), 1)
    sub = lax.broadcasted_iota(jnp.int32, (8, LANES), 0)
    slab_row = lax.broadcasted_iota(jnp.int32, (CY, NZ), 0)
    slab_col = lax.broadcasted_iota(jnp.int32, (CY, NZ), 1)
    base = (cz % 4) * 32

    def remote(a, b, send, recv, dev):
        return pltpu.make_async_remote_copy(
            src_ref=a, dst_ref=b, send_sem=send, recv_sem=recv, device_id=dev, device_id_type=MESH
        )

    def await_bytes(ref, sem):
        pltpu.make_async_copy(ref, ref, sem).wait()

    loads[6].wait()
    depth = lax.broadcasted_iota(jnp.int32, (KB, NZ), 1)
    length = jnp.broadcast_to(ext[...], (KB, KB)).astype(F32)
    earlier = lax.broadcasted_iota(jnp.int32, (KB, KB), 1) < lax.broadcasted_iota(jnp.int32, (KB, KB), 0)
    not_later = lax.broadcasted_iota(jnp.int32, (KB, KB), 1) <= lax.broadcasted_iota(jnp.int32, (KB, KB), 0)
    begins = jnp.sum(jnp.where(earlier, length, 0.0), axis=1, keepdims=True)
    ends = jnp.sum(jnp.where(not_later, length, 0.0), axis=1, keepdims=True)
    depth = depth.astype(F32)
    own_onehot = jnp.where((depth >= begins) & (depth < ends), 1.0, 0.0).astype(F32)
    onehot[1] = own_onehot

    def restrict_row(planes, base):
        spread = jnp.zeros((8, LANES), F32)
        for f in range(4):
            total = jnp.sum(planes[f], axis=0, keepdims=True)
            value = jnp.sum(total * onehot[1], axis=1, keepdims=True)
            spread = spread + jnp.where(lane == base + 8 * f + sub, value, 0.0)
        return jnp.sum(spread, axis=0, keepdims=True) * (1.0 / SLAB_CELLS)

    loads[0].wait()
    loads[1].wait()

    def masked(x, carry):
        for i in range(2):
            value = cond[i, x] * jnp.where(phase[x] == i + 1, 1.0, LOW_COND)
            cd[i, x + 1] = value
            syc[0, i, pl.ds(x, 1), :] = value[0:1]
            syc[1, i, pl.ds(x, 1), :] = value[CY - 1 : CY]
        return carry

    lax.fori_loop(0, CX, masked, 0)

    loads[2].wait()

    def plane_of(x, carry):
        return tuple(carry[f] + r[f, x, 0:8] + r[f, x, 8:16] for f in range(4))

    planes = lax.fori_loop(0, CX, plane_of, tuple(jnp.zeros((8, NZ), F32) for _ in range(4)))
    row_z[...] = restrict_row(planes, base)
    loads[3].wait()

    pl.semaphore_wait(barrier, len(greeted))

    started = []

    def go(copy):
        copy.start()
        started.append(copy)
        return copy

    for dev in along_z:
        remote(row_z, slots_z.at[pl.ds(cz, 1)], p0_send.at[0], p0_recv.at[0], dev).start()
    pltpu.make_async_copy(row_z, slots_z.at[pl.ds(cz, 1)], p0_recv.at[0]).start()
    cond_up = go(remote(cd.at[:, CX], hxc.at[0], near_send.at[0], near_recv.at[0], up))
    cond_down = go(remote(cd.at[:, 1], hxc.at[1], near_send.at[1], near_recv.at[1], down))
    cond_right = go(remote(syc.at[1], hyc.at[0], near_send.at[2], near_recv.at[2], right))
    cond_left = go(remote(syc.at[0], hyc.at[1], near_send.at[3], near_recv.at[3], left))
    hot_up = go(remote(onehot.at[1], onehot.at[0], near_send.at[4], near_recv.at[4], up))
    hot_down = go(remote(onehot.at[1], onehot.at[2], near_send.at[5], near_recv.at[5], down))
    cinv_up = go(remote(cinv.at[1], cinv.at[0], near_send.at[6], near_recv.at[6], up))
    cinv_down = go(remote(cinv.at[1], cinv.at[2], near_send.at[7], near_recv.at[7], down))

    loads[4].wait()
    loads[5].wait()

    def rates(x, carry):
        mask = inter[x].astype(F32)
        cr[x] = adm[0, x] * mask
        sr[x] = adm[1, x] * mask
        return carry

    lax.fori_loop(0, CX, rates, 0)
    for f in range(4):
        for edge in (0, CX + 1):
            first[f, edge] = jnp.zeros((CY, NZ), F32)
            second[0, f, edge] = jnp.zeros((CY, NZ), F32)
            second[1, f, edge] = jnp.zeros((CY, NZ), F32)

    inside = [
        jnp.where(brick > 0, 1.0, 0.0).astype(F32), jnp.where(brick < 31, 1.0, 0.0).astype(F32),
        jnp.where(grp > 0, 1.0, 0.0).astype(F32), jnp.where(grp < 7, 1.0, 0.0).astype(F32),
    ]
    for copy in (cond_up, cond_down, cond_right, cond_left):
        copy.wait_recv()
    for i in range(2):
        cd[i, 0] = hxc[0, i] * inside[0]
        cd[i, CX + 1] = hxc[1, i] * inside[1]

    def weigh(x, carry):
        out_low = jnp.where((x == 0) & (brick == 0), 1.0, 0.0).astype(F32)
        out_high = jnp.where((x == CX - 1) & (brick == 31), 1.0, 0.0).astype(F32)
        charge = cr[x]
        for i in range(2):
            here = cd[i, x + 1]
            low = 0.5 * (here + cd[i, x])
            high = 0.5 * (here + cd[i, x + 2])
            before = hyc[0, i, pl.ds(x, 1), :] * inside[2]
            after = hyc[1, i, pl.ds(x, 1), :] * inside[3]
            ym = 0.5 * (here + jnp.where(slab_row == 0, before, roll(here, 1, 0)))
            yp = 0.5 * (here + jnp.where(slab_row == CY - 1, after, roll(here, -1, 0)))
            zm = 0.5 * (here + jnp.where(slab_col == 0, 0.0, roll(here, 1, 1)))
            zp = 0.5 * (here + jnp.where(slab_col == NZ - 1, 0.0, roll(here, -1, 1)))
            total = low + high + ym + yp + zm + zp + EPS_SHIFT
            tw[i, x] = total
            dinv[i, x] = 1.0 / (total + charge)
            ee[i, x] = (
                EPS_SHIFT + zm + zp + out_low * low + out_high * high
                + jnp.where(slab_row == 0, ym, 0.0) * (1.0 - inside[2])
                + jnp.where(slab_row == CY - 1, yp, 0.0) * (1.0 - inside[3])
            )
            wx[i, x] = low * (1.0 - out_low)
            wx[i, x + 1] = high * (1.0 - out_high)
            wyb[0, i, pl.ds(x, 1), :] = ym[0:1] * inside[2]
            wyb[1, i, pl.ds(x, 1), :] = yp[CY - 1 : CY] * inside[3]
            wym[i, x] = jnp.where(slab_row == 0, 0.0, ym)
            wyp[i, x] = jnp.where(slab_row == CY - 1, 0.0, yp)
            wzm[i, x] = jnp.where(slab_col == 0, 0.0, zm)
            wzp[i, x] = jnp.where(slab_col == NZ - 1, 0.0, zp)
        return carry

    ends = lambda n: n + 4 * (n // 2)
    lax.fori_loop(0, 4, lambda n, c: weigh(ends(n), c), 0)

    def around(v, f, x, center):
        i = f // 2
        return (
            wx[i, x] * v[f, x] + wx[i, x + 1] * v[f, x + 2]
            + wym[i, x] * roll(center, 1, 0) + wyp[i, x] * roll(center, -1, 0)
            + wzm[i, x] * roll(center, 1, 1) + wzp[i, x] * roll(center, -1, 1)
        )

    def smoother(given, k):
        out = second.at[k % 2]

        def scaled(x, carry):
            for f in range(4):
                first[f, x + 1] = given[f, x] * dinv[f // 2, x]
            return carry

        def stencil(x, carry):
            v = [first[f, x + 1] for f in range(4)]
            real, imag = sr[x] * (v[0] - v[2]), sr[x] * (v[1] - v[3])
            swirl = (imag, -real, -imag, real)
            for f in range(4):
                value = v[f] + dinv[f // 2, x] * (around(first, f, x, v[f]) + cr[x] * v[f ^ 2] + swirl[f])
                out[f, x + 1] = value
                sy[k, 0, f, pl.ds(x, 1), :] = value[0:1]
                sy[k, 1, f, pl.ds(x, 1), :] = value[CY - 1 : CY]
            return carry

        halos = [
            remote(out.at[:, CX], hx.at[k, 0], halo_sem.at[k, 0, 0], halo_sem.at[k, 1, 0], up),
            remote(out.at[:, 1], hx.at[k, 1], halo_sem.at[k, 0, 1], halo_sem.at[k, 1, 1], down),
        ]
        sides = [
            remote(sy.at[k, 1], hy.at[k, 0], halo_sem.at[k, 0, 2], halo_sem.at[k, 1, 2], right),
            remote(sy.at[k, 0], hy.at[k, 1], halo_sem.at[k, 0, 3], halo_sem.at[k, 1, 3], left),
        ]

        def edges():
            lax.fori_loop(0, 4, lambda n, c: scaled(ends(n), c), 0)
            lax.fori_loop(0, 2, lambda n, c: stencil(n * (CX - 1), c), 0)

        def send():
            for copy in halos:
                copy.start()

        def interior():
            lax.fori_loop(2, CX - 2, scaled, 0)
            lax.fori_loop(1, CX - 1, stencil, 0)
            for copy in sides:
                copy.start()
            return halos + sides

        return edges, send, interior

    def operate(k):
        v = second.at[k % 2]

        def stencil(x, carry):
            c = [v[f, x + 1] for f in range(4)]
            over_real, over_imag = c[0] - c[2], c[1] - c[3]
            real = cr[x] * over_real - sr[x] * over_imag
            imag = cr[x] * over_imag + sr[x] * over_real
            flow = (real, imag, -real, -imag)
            for f in range(4):
                u[f, x] = tw[f // 2, x] * c[f] - around(v, f, x, c[f]) + flow[f]
            return carry

        lax.fori_loop(0, CX, stencil, 0)

    def receive_halos(k, copies):
        for copy in copies[2:]:
            copy.wait_recv()

        def rows(x, carry):
            for f in range(4):
                for side, y in ((0, 0), (1, CY - 1)):
                    u[f, x, y : y + 1, :] = u[f, x, y : y + 1, :] - (
                        wyb[side, f // 2, pl.ds(x, 1), :] * hy[k, side, f, pl.ds(x, 1), :]
                    )
            return carry

        lax.fori_loop(0, CX, rows, 0)
        for copy in copies[:2]:
            copy.wait_recv()
        for copy in copies:
            copy.wait_send()

    def correct(k, coarse):
        profile = []
        for j in range(3):
            per_field = []
            for f in range(4):
                product = jnp.zeros((8, LANES), F32)
                for s in range(8):
                    product = product + cinv[j, 8 * f : 8 * f + 8, LANES * s : LANES * s + LANES] * coarse[s]
                value = jnp.sum(product, axis=1, keepdims=True)
                per_field.append(jnp.sum(value * onehot[j], axis=0, keepdims=True))
            profile.append(per_field)
        own = profile[1]
        rows = own + [roll(own[f], 1, 1) for f in range(4)] + [roll(own[f], -1, 1) for f in range(4)]
        rows = rows + [own[0] - own[2], own[1] - own[3]]
        for n, value in enumerate(rows):
            table[n] = jnp.broadcast_to(value, (8, NZ))
        for f in range(4):
            u[f, 0] = u[f, 0] - wx[f // 2, 0] * (hx[k, 0, f] + (profile[0][f] - own[f]))
            u[f, CX - 1] = u[f, CX - 1] - wx[f // 2, CX] * (hx[k, 1, f] + (profile[2][f] - own[f]))

    def advance(k, alpha):
        zero = jnp.zeros((8, LANES), F32)

        def tile(t, dots):
            lanes = pl.ds(pl.multiple_of(LANES * t, LANES), LANES)
            p = [table[n, :, lanes] for n in range(14)]

            def step(x, carry):
                ri, ii, *sums = carry
                for half in range(2):
                    at = (x, slice(8 * half, 8 * half + 8), lanes)
                    charge, storage = cr[at], sr[at]
                    real = charge * p[12] - storage * p[13]
                    imag = charge * p[13] + storage * p[12]
                    flow = (real, imag, -real, -imag)
                    for f in range(4):
                        i = f // 2
                        raised = u[(f,) + at] + (
                            ee[(i,) + at] * p[f] - wzm[(i,) + at] * p[4 + f] - wzp[(i,) + at] * p[8 + f] + flow[f]
                        )
                        left_over = r[(f,) + at]
                        if k > 0:
                            old = q[(f,) + at]
                            left_over = left_over - alpha * old
                            r[(f,) + at] = left_over
                            raised = old - alpha * raised
                        q[(f,) + at] = raised
                        ri = ri + left_over * raised
                        ii = ii + raised * raised
                        sums[f] = sums[f] + raised
                return (ri, ii, *sums)

            ri, ii, *sums = lax.fori_loop(0, CX, step, (*dots, zero, zero, zero, zero), unroll=4)
            for f in range(4):
                total[f, :, lanes] = sums[f]
            return ri, ii

        ri, ii = lax.fori_loop(0, TILES, tile, (zero, zero))
        return ri, ii, total

    def update_search(k, alpha):
        smoothed = second.at[k % 2]

        def step(x, carry):
            for f in range(4):
                put = smoothed[f, x + 1] + jnp.concatenate([table[f], table[f]], axis=0)
                if k == 0:
                    z[f, x] = put
                else:
                    old = z[f, x]
                    sol[f, x] = alpha * old if k == 1 else sol[f, x] + alpha * old
                    z[f, x] = old - alpha * put
            return carry

        lax.fori_loop(0, CX, step, 0)

    slot = (cz % 4) * 32 + cx * 8 + cy * 2 + cz // 4
    sibling = {"brick": brick, "grp": cx * 2 + 1 - core}

    def share(k, ri, ii, planes, edges, send_halos):
        coarse = restrict_row(planes, 0) if k < ITERS - 1 else jnp.zeros((1, LANES), F32)
        ri = jnp.sum(jnp.sum(ri, axis=0, keepdims=True), axis=1, keepdims=True)
        ii = jnp.sum(jnp.sum(ii, axis=0, keepdims=True), axis=1, keepdims=True)
        row_c[k] = jnp.where(lane[0:1] < 32, coarse, jnp.where(lane[0:1] < 64, ri, ii))
        copy = remote(row_c.at[k], slots_c.at[k], core_sem.at[k, 0], core_sem.at[k, 1], sibling)
        copy.start()
        edges()
        copy.wait_recv()
        row_all[k] = row_c[k] + slots_c[k]

        def send(by, bx):
            remote(
                row_all.at[k], slots_all.at[k, pl.ds(slot, 1)], all_send.at[k], all_recv.at[k],
                {"brick": by, "grp": bx},
            ).start()

        def far(n, carry):
            half = (n + 1) // 2
            dz = 4 + half * (1 - 2 * (n % 2))
            bz = (cz + dz) % 8
            for dy, dx in far_first:
                send(ys[dy] + bz, xs[dx] + core)
            return carry

        lax.fori_loop(0, 7, far, 0)
        for dy, dx in far_first[:-1]:
            send(ys[dy] + cz, xs[dx] + core)
        pltpu.make_async_copy(
            row_all.at[k], slots_all.at[k, pl.ds(slot, 1)], all_recv.at[k]
        ).start()
        send_halos()
        return copy

    def gather(k):
        await_bytes(slots_all.at[k], all_recv.at[k])
        quarters = []
        for n in range(4):
            rows = slots_all[k, 32 * n : 32 * n + 8]
            for m in range(1, 4):
                rows = rows + slots_all[k, 32 * n + 8 * m : 32 * n + 8 * m + 8]
            quarters.append(rows)
        dots = jnp.sum(quarters[0] + quarters[1] + quarters[2] + quarters[3], axis=0, keepdims=True)
        alpha = (roll(dots, 64, 1) / (dots + 1e-6))[:, LANES - 1 :]
        quarters = [jnp.where(lane < 32, rows, 0.0) for rows in quarters]
        rows = quarters[0] + roll(quarters[1], 32, 1) + roll(quarters[2], 64, 1) + roll(quarters[3], 96, 1)
        return [rows[s : s + 1] for s in range(8)], jnp.broadcast_to(alpha, (1, LANES))

    def pass_on():
        await_bytes(slots_z, p0_recv.at[0])
        row_p[0] = jnp.sum(slots_z[0:4], axis=0, keepdims=True)
        row_p[1] = jnp.sum(slots_z[4:8], axis=0, keepdims=True)
        mine = slots_p.at[pl.ds(2 * cy, 2), pl.ds(grp, 1)]
        for dev in plane:
            remote(row_p, mine, p0_send.at[1], p0_recv.at[1], dev).start()
        pltpu.make_async_copy(row_p, mine, p0_recv.at[1]).start()
        lax.fori_loop(2, CX - 2, weigh, 0)

    edges, send_halos, interior = smoother(r, 0)
    edges()
    send_halos()
    pass_on()
    halos = interior()
    operate(0)
    receive_halos(0, halos)
    for copy in (hot_up, hot_down, cinv_up, cinv_down):
        copy.wait_recv()
    await_bytes(slots_p, p0_recv.at[1])
    coarse = [jnp.sum(slots_p[s], axis=0, keepdims=True) for s in range(8)]
    alpha = None
    cores = []
    for k in range(ITERS):
        correct(k, coarse)
        ri, ii, planes = advance(k, None if k == 0 else jnp.broadcast_to(alpha, (8, LANES)))
        edges, send_halos, interior = smoother(q, k + 1) if k < ITERS - 1 else (lambda: None,) * 3
        cores.append(share(k, ri, ii, planes, edges, send_halos))
        wide = None if k == 0 else jnp.broadcast_to(jnp.concatenate([alpha] * TILES, axis=1), (CY, NZ))
        if k < ITERS - 1:
            halos = interior()
        update_search(k, wide)
        if k < ITERS - 1:
            operate(k + 1)
            receive_halos(k + 1, halos)
        coarse, alpha = gather(k)

    last_alpha[0, 0] = jnp.broadcast_to(jnp.concatenate([alpha] * TILES, axis=1), (CY, NZ))
    for copy in started + cores:
        copy.wait_send()
    await_bytes(sizes.at[pl.ds(0, 7)], p0_send.at[0])
    await_bytes(sizes.at[pl.ds(0, 62)], p0_send.at[1])
    for k in range(ITERS):
        await_bytes(sizes, all_send.at[k])


def local(source, phase_label, interface, conductivity, admittance, extents, coarse_inverse):
    block = (CX, CY, NZ)
    padded = (CX + 2, CY, NZ)
    vmem = lambda *shape: pltpu.VMEM(shape, F32)
    ints = pltpu.VMEM(block, jnp.int32)
    dma = lambda *shape: pltpu.SemaphoreType.DMA(shape)
    scratch = [
        vmem(4, *block),
        vmem(4, *padded), vmem(2, 4, *padded), vmem(2, *block), ints, ints, vmem(2, *block),
        vmem(2, *padded), vmem(*block), vmem(*block),
        vmem(2, CX + 1, CY, NZ), vmem(2, *block), vmem(2, *block), vmem(2, *block), vmem(2, *block),
        vmem(2, *block), vmem(2, *block), vmem(2, *block), vmem(2, 2, CX, NZ),
        vmem(3, 4 * KB, 1024), vmem(3, KB, NZ), vmem(14, 8, NZ),
        vmem(2, 2, CY, NZ), vmem(2, 2, CX, NZ), vmem(2, 2, CX, NZ),
        vmem(3, 2, 4, CY, NZ), vmem(3, 2, 4, CX, NZ), vmem(3, 2, 4, CX, NZ),
        vmem(1, LANES), vmem(8, LANES), vmem(2, 1, LANES), vmem(8, 8, LANES),
        vmem(3, 1, LANES), vmem(3, 1, LANES), vmem(3, 1, LANES), vmem(3, 128, LANES), vmem(127, 1, LANES),
        pltpu.VMEM((1, KB), jnp.int32), vmem(4, 8, NZ),
        dma(7), dma(8), dma(8), dma(1), dma(3, 2, 4), dma(3), dma(3), dma(3, 2), dma(3), dma(3),
    ]
    hbm = pl.BlockSpec(memory_space=pl.ANY)
    out = pltpu.VMEM((4, *block), F32)
    in_vmem = pl.BlockSpec(memory_space=pltpu.VMEM)
    iterate, search, residual, image, alpha = pl.pallas_call(
        kernel,
        out_shape=(out, out, out, out, pltpu.VMEM((1, 1, CY, NZ), F32)),
        in_specs=[hbm] * 7,
        out_specs=(in_vmem,) * 5,
        scratch_shapes=scratch,
        compiler_params=pltpu.CompilerParams(
            collective_id=0, has_side_effects=True, vmem_limit_bytes=59 * 1024 * 1024
        ),
    )(extents, source, phase_label, interface, conductivity, admittance, coarse_inverse)
    return iterate + alpha * search, residual - alpha * image


def solution(mesh):
    placed = (
        P(None, "brick", "grp", None),
        P("brick", "grp", None),
        P("brick", "grp", None),
        P(None, "brick", "grp", None),
        P(None, "brick", "grp", None),
        P("brick", None),
        P("brick", None),
    )
    return jax.shard_map(
        local,
        mesh=mesh,
        in_specs=placed,
        out_specs=(P(None, "brick", "grp", None), P(None, "brick", "grp", None)),
        check_vma=False,
    )
```
